256 devices in a mesh: head: 16 (over x, z_lo), ans: 16 (over y, z_hi, core).
Axes of the slice: x: 4, y: 4, z: 8 (z_hi: 2, z_lo: 4; z = z_hi * 4 + z_lo), core: 2. Of those that a mesh axis runs over, the one named last changes fastest.
Arguments:
- query_nope: bfloat16 [2048, 16384], P('ans', 'head'), may hold values from -6 to 6
- query_rope: bfloat16 [2048, 8192], P('ans', 'head')
- answer_latent: bfloat16 [2048, 576], P('ans'), may hold values from -6 to 6
- prompt_latent: bfloat16 [1536, 576], P('ans')
- weight_uk: bfloat16 [128, 128, 512], P('head'), may hold values from -0.5 to 0.5
- weight_uv: bfloat16 [128, 512, 128], P('head'), may hold values from -0.25 to 0.25
- grad_heads: bfloat16 [2048, 16384], P('ans', 'head'), may hold values from -6 to 6
- valid_tokens: int32 [32], P('ans'), may hold values from 16 to 64, as said below
Outputs:
- d_query_nope: bfloat16 [2048, 16384], P('ans', 'head')
- d_query_rope: bfloat16 [2048, 8192], P('ans', 'head')
- d_answer_latent: float32 [2048, 576], P('ans')
- d_prompt_latent: float32 [1536, 576], P('ans')
- d_weight_uk: float32 [128, 128, 512], P('head', 'ans')
- d_weight_uv: float32 [128, 512, 128], P('head', 'ans')
The draws below stay inside these ranges and needn't reach their ends.
Inputs may be any that keep to these rules, and one draw needn't show every extreme that they name: `valid_tokens`: every block has at least 16 valid tokens; some block is full and some has exactly 16.
All inputs are finite; a program needn't handle non-finite values.
Results may differ from the reference program's by a relative error of at most 0.035.
Values may be sent and summed in bfloat16 or wider, within the bound.
A program may use at most 64 MiB of HBM per device.

```python
import jax
import jax.numpy as jnp
from jax import lax

LAT = 512
ROPE = 64
HD = 128
VD = 128
GROUP = 64
HEADS = 128
ANSWERS = 32
TOKENS = 2048
PROMPT = 1536


def draw_prompt_latent(key, part):
    key = jax.random.fold_in(key, 1)
    latent = jax.random.normal(key, (PROMPT, LAT + ROPE), jnp.float32)
    return latent.astype(jnp.bfloat16)


def draw_query_rope(key, part):
    key = jax.random.fold_in(key, 2)
    rotary = jax.random.normal(key, (TOKENS, HEADS, ROPE), jnp.float32)
    return rotary.reshape(TOKENS, HEADS * ROPE).astype(jnp.bfloat16)


def draw_valid_tokens(key, part):
    key = jax.random.fold_in(key, 3)
    counts = jax.random.randint(key, (ANSWERS,), GROUP // 4, GROUP + 1, jnp.int32)
    return counts.at[0].set(GROUP).at[1].set(GROUP // 4)


def block_levels(rng, dims, pieces, smallest, high):
    level, own = 1.0, jax.random.fold_in(rng, 6)
    for dim, blocks in pieces:
        heights = jnp.exp(jax.random.uniform(jax.random.fold_in(own, dim), (blocks,), jnp.float32, smallest / len(pieces), high / len(pieces)))
        level = level * jnp.repeat(heights, dims[dim] // blocks).reshape([-1 if axis == dim else 1 for axis in range(len(dims))])
    return level


def bell_draw(stream_key, shape, deviation, most, cuts=(), held_as=jnp.bfloat16):
    result = jax.random.normal(stream_key, shape, jnp.float32) * deviation
    if len(cuts) > 0:
        result = block_levels(stream_key, shape, cuts, -0.22, 0.18) * result
    return jnp.clip(result, min=-most, max=most).astype(held_as)


def setup_inputs(seed: int = 0) -> dict:
    key_of = jax.random.split(jax.random.key(seed), 9)
    return {
        "query_nope": bell_draw(key_of[0], (TOKENS, HEADS * HD), 1.0, 6.0, ((0, 16), (1, 16))),
        "query_rope": draw_query_rope(jax.random.fold_in(key_of[8], 71), 0),
        "answer_latent": bell_draw(key_of[2], (TOKENS, LAT + ROPE), 1.0, 6.0, ((0, 16),)),
        "prompt_latent": draw_prompt_latent(jax.random.fold_in(key_of[8], 71), 0),
        "weight_uk": bell_draw(key_of[4], (HEADS, HD, LAT), HD ** -0.5, 0.5, ((0, 16),)),
        "weight_uv": bell_draw(key_of[5], (HEADS, LAT, VD), LAT ** -0.5, 0.25, ((0, 16),)),
        "grad_heads": bell_draw(key_of[6], (TOKENS, HEADS * VD), 1.0, 6.0, ((0, 16), (1, 16))),
        "valid_tokens": draw_valid_tokens(jax.random.fold_in(key_of[8], 71), 0),
    }


def head_terms(nope_head, rope_head, grad_head, weight_k, weight_v, prompt, own_keys, valid_tokens):
    softmax_scale = (HD + ROPE) ** -0.5
    answers = own_keys.shape[0]
    key_width = LAT + ROPE
    latent_query = jnp.dot(nope_head, weight_k, preferred_element_type=jnp.float32).astype(jnp.bfloat16)
    queries = jnp.concatenate([latent_query, rope_head], axis=1)
    far_scores = jnp.dot(queries, prompt.T, preferred_element_type=jnp.float32) * softmax_scale
    query_blocks = queries.reshape(answers, GROUP, key_width)
    own_scores = jnp.einsum("aik,ajk->aij", query_blocks.astype(jnp.float32), own_keys.astype(jnp.float32)) * softmax_scale
    position = jnp.arange(GROUP)
    allowed = (position[None, None, :] <= position[None, :, None]) & (position[None, None, :] < valid_tokens[:, None, None])
    own_scores = jnp.where(allowed, own_scores, -1e30)
    top = jnp.maximum(jnp.max(far_scores, axis=1), jnp.max(own_scores, axis=2).reshape(-1))
    far_exp = jnp.exp(far_scores - top[:, None])
    own_exp = jnp.where(allowed, jnp.exp(own_scores - top.reshape(answers, GROUP)[:, :, None]), 0.0)
    total = jnp.sum(far_exp, axis=1) + jnp.sum(own_exp, axis=2).reshape(-1)
    far_prob = far_exp / total[:, None]
    own_prob = own_exp / total.reshape(answers, GROUP)[:, :, None]
    far_low = far_prob.astype(jnp.bfloat16)
    own_low = own_prob.astype(jnp.bfloat16)
    values = prompt[:, :LAT]
    own_values = own_keys[:, :, :LAT]
    latent_out = (jnp.dot(far_low, values, preferred_element_type=jnp.float32)
                  + jnp.einsum("aij,ajl->ail", own_low.astype(jnp.float32), own_values.astype(jnp.float32)).reshape(-1, LAT)).astype(jnp.bfloat16)
    live_rows = (position[None, :] < valid_tokens[:, None]).reshape(-1)
    grad_live = jnp.where(live_rows[:, None], grad_head, jnp.zeros_like(grad_head))
    grad_wv = jnp.dot(latent_out.T, grad_live, preferred_element_type=jnp.float32)
    grad_latent = jnp.dot(grad_live, weight_v.T, preferred_element_type=jnp.float32).astype(jnp.bfloat16)
    delta = jnp.sum(grad_latent.astype(jnp.float32) * latent_out.astype(jnp.float32), axis=1)
    grad_far = jnp.dot(grad_latent, values.T, preferred_element_type=jnp.float32)
    grad_blocks = grad_latent.reshape(answers, GROUP, LAT)
    grad_own = jnp.einsum("ail,ajl->aij", grad_blocks.astype(jnp.float32), own_values.astype(jnp.float32))
    far_grad_scores = (far_prob * (grad_far - delta[:, None]) * softmax_scale).astype(jnp.bfloat16)
    own_grad_scores = (own_prob * (grad_own - delta.reshape(answers, GROUP)[:, :, None]) * softmax_scale).astype(jnp.bfloat16)
    grad_queries = (jnp.dot(far_grad_scores, prompt, preferred_element_type=jnp.float32)
                    + jnp.einsum("aij,ajk->aik", own_grad_scores.astype(jnp.float32), own_keys.astype(jnp.float32)).reshape(-1, key_width))
    grad_lq = grad_queries[:, :LAT].astype(jnp.bfloat16)
    grad_rope = grad_queries[:, LAT:].astype(jnp.bfloat16)
    grad_nope = jnp.dot(grad_lq, weight_k.T, preferred_element_type=jnp.float32).astype(jnp.bfloat16)
    grad_wk = jnp.dot(nope_head.T, grad_lq, preferred_element_type=jnp.float32)
    prompt_keys = jnp.dot(far_grad_scores.T, queries, preferred_element_type=jnp.float32)
    prompt_values = jnp.dot(far_low.T, grad_latent, preferred_element_type=jnp.float32)
    grad_prompt = prompt_keys + jnp.pad(prompt_values, ((0, 0), (0, ROPE)))
    own_key_grad = jnp.einsum("aij,aik->ajk", own_grad_scores.astype(jnp.float32), query_blocks.astype(jnp.float32))
    own_value_grad = jnp.einsum("aij,ail->ajl", own_low.astype(jnp.float32), grad_blocks.astype(jnp.float32))
    grad_own_keys = (own_key_grad + jnp.pad(own_value_grad, ((0, 0), (0, 0), (0, ROPE)))).reshape(-1, key_width)
    return grad_nope, grad_rope, grad_wk, grad_wv, grad_prompt, grad_own_keys


def reference(query_nope, query_rope, answer_latent, prompt_latent, weight_uk, weight_uv, grad_heads, valid_tokens):
    tokens = query_nope.shape[0]
    nope_split = query_nope.reshape(tokens, HEADS, HD).transpose(1, 0, 2)
    rope_split = query_rope.reshape(tokens, HEADS, ROPE).transpose(1, 0, 2)
    grad_split = grad_heads.reshape(tokens, HEADS, VD).transpose(1, 0, 2)
    own_keys = answer_latent.reshape(ANSWERS, GROUP, LAT + ROPE)

    def one_head(carry, inputs):
        nope_head, rope_head, grad_head, weight_k, weight_v = inputs
        grad_nope, grad_rope, grad_wk, grad_wv, grad_prompt, grad_own_keys = head_terms(
            nope_head, rope_head, grad_head, weight_k, weight_v, prompt_latent, own_keys, valid_tokens)
        return (carry[0] + grad_prompt, carry[1] + grad_own_keys), (grad_nope, grad_rope, grad_wk, grad_wv)

    start = (jnp.zeros((PROMPT, LAT + ROPE), jnp.float32), jnp.zeros((tokens, LAT + ROPE), jnp.float32))
    sums, stacked = lax.scan(one_head, start, (nope_split, rope_split, grad_split, weight_uk, weight_uv))
    grad_prompt, grad_answer = sums
    grad_nope, grad_rope, grad_wk, grad_wv = stacked
    d_query_nope = grad_nope.transpose(1, 0, 2).reshape(tokens, HEADS * HD)
    d_query_rope = grad_rope.transpose(1, 0, 2).reshape(tokens, HEADS * ROPE)
    return (d_query_nope, d_query_rope, grad_answer, grad_prompt, grad_wk, grad_wv)
```

```python
import jax
import jax.numpy as jnp
from jax import lax
from jax.experimental import pallas as pl
from jax.experimental.pallas import tpu as pltpu
from jax.sharding import PartitionSpec as P

LAT = 512
ROPE = 64
HD = 128
VD = 128
GROUP = 64
W = LAT + ROPE
MESH = pl.DeviceIdType.MESH
F32 = jnp.float32
BF = jnp.bfloat16
SCALE = (HD + ROPE) ** (-0.5)

T = 128
H = 8
R = T * H
SH = 96
KP = 1536
KA = KP + T
PAIR = 2 * T


def nn(a, b):
    return jnp.dot(a, b, preferred_element_type=F32)


def nt(a, b):
    return lax.dot_general(a, b, (((1,), (1,)), ((), ())), preferred_element_type=F32)


def kernel(
    nope, rope, ans, prm, wuk, wuv, gh, valid,
    o_nope, o_rope, o_ans, o_prm, o_wk, o_wv,
    kall, kt, q, glt, gl, s, gp, p, ds, mx, g,
    gs, gcr, xs, xacc, xr1, xs2, xr2, ysum, ys, yr, zs, zr, fz, ag,
    as_, ar, fa, aa,
    wvt, wvs, wvc, wvacc, wvy, wv1, wv2s, wv2r, wvz, wvzs, wvzr,
    wkt, wks, wkc, wkacc, wky, wk1, wk2s, wk2r, wkz, wkzs, wkzr,
    sy, ry, sz, rz, sx, rx, scc, rcc,
    sgc, rgc, sx1, rx1, sx2, rx2, syy, ryy, szz, rzz, sag, rag,
    sa1, ra1, sa2, ra2,
    swv, rwv, swk, rwk,
):
    h = lax.axis_index("head")
    a = lax.axis_index("ans")
    x, zl = h // 4, h % 4
    y, zh, c = a // 4, (a // 2) % 2, a % 2
    oc, ozh = 1 - c, 1 - zh
    par = x % 2
    x1 = x + 1 - 2 * par
    x3 = 3 - x
    y1 = y + 1 - 2 * (y % 2)
    y3 = 3 - y

    def dev(x_, y_, zh_, zl_, c_):
        return {"head": x_ * 4 + zl_, "ans": y_ * 4 + zh_ * 2 + c_}

    sib = dev(x, y, zh, zl, oc)

    def rc(src, dst, ss, rs, d):
        return pltpu.make_async_remote_copy(
            src_ref=src, dst_ref=dst, send_sem=ss, recv_sem=rs, device_id=d, device_id_type=MESH
        )

    def arrived(dst, rs):
        rc(dst, dst, rs, rs, sib).wait_recv()

    def sent(src, ss):
        rc(src, src, ss, ss, sib).wait_send()

    bar = pltpu.get_barrier_semaphore()
    count = 0
    for i in range(1, 16):
        pl.semaphore_signal(bar, inc=1, device_id={"head": (h + i) % 16, "ans": a}, device_id_type=MESH)
        count += 1
    for i in range(1, 4):
        pl.semaphore_signal(bar, inc=1, device_id=dev(x, (y + i) % 4, zh, zl, c), device_id_type=MESH)
        count += 1
    for i in range(4):
        pl.semaphore_signal(bar, inc=1, device_id=dev(x, y, ozh, i, c), device_id_type=MESH)
        count += 1
    pl.semaphore_signal(bar, inc=1, device_id=sib, device_id_type=MESH)
    count += 1
    pl.semaphore_wait(bar, count)

    def rows(y_, zh_, c_, half=None):
        base = (y_ * 4 + zh_ * 2 + c_) * SH
        if half is None:
            return kall.at[pl.ds(pl.multiple_of(base, 16), SH)]
        return kall.at[pl.ds(pl.multiple_of(base + half * 48, 16), 48)]

    own_half = prm.at[pl.ds(pl.multiple_of(par * 48, 16), 48)]

    def yk(k):
        return (y + k) % 4

    def y_send(zr_, k):
        zz = zh if zr_ == 0 else ozh
        src = own_half if zr_ == 0 else rows(y, zz, c, par)
        return rc(src, rows(y, zz, c, par), sy.at[zr_ * 3 + k - 1], ry.at[zr_ * 3 + k - 1],
                  dev(x, yk(k), zh, zl, c))

    def y_wait(zr_, k):
        zz = zh if zr_ == 0 else ozh
        arrived(rows((y + 4 - k) % 4, zz, c, par), ry.at[zr_ * 3 + k - 1])

    def x_send(zr_, k):
        yy = yk(k)
        zz = zh if zr_ == 0 else ozh
        xt = (x + 1 + 2 * (yy % 2)) % 4
        view = rows(yy, zz, c, par)
        return rc(view, view, sx.at[zr_ * 4 + k], rx.at[zr_ * 4 + k], dev(xt, y, zh, zl, c))

    def x_wait(zr_, k):
        zz = zh if zr_ == 0 else ozh
        arrived(rows(yk(k), zz, c, 1 - par), rx.at[zr_ * 4 + k])

    def c_send(zr_, k, second):
        zz = zh if zr_ == 0 else ozh
        half = (1 - par) if second else par
        view = rows(yk(k), zz, c, half)
        i = (zr_ * 4 + k) * 2 + second
        return rc(view, view, scc.at[i], rcc.at[i], sib)

    def c_wait(zr_, k, second):
        zz = zh if zr_ == 0 else ozh
        half = (1 - par) if second else par
        i = (zr_ * 4 + k) * 2 + second
        arrived(rows(yk(k), zz, oc, half), rcc.at[i])

    def z_copy(to_zl, i):
        return rc(own_half, rows(y, zh, c, par), sz.at[i], rz.at[0], dev(x, y, ozh, to_zl, c))

    @pl.when(zl == 3)
    def _():
        z_copy(0, 0).start()
        z_copy(1, 1).start()

    @pl.when(zl == 0)
    def _():
        z_copy(3, 0).start()
        z_copy(2, 1).start()

    for k in (1, 3, 2):
        y_send(0, k).start()
    own = pltpu.make_async_copy(prm, rows(y, zh, c), sz.at[2])
    own.start()
    own.wait()
    c_send(0, 0, 0).start()
    c_send(0, 0, 1).start()
    kall[KP:KA, :] = ans[...]

    v0, v1 = valid[0], valid[1]
    tok = lax.broadcasted_iota(jnp.int32, (T, T), 0)
    live = (tok % GROUP < jnp.where(tok < GROUP, v0, v1)).astype(F32)

    def project(i, _):
        for hh in range(2):
            hd = 2 * i + hh
            lanes = pl.ds(pl.multiple_of(hd * T, T), T)
            qrows = pl.ds(pl.multiple_of(hd * T, T), T)
            q[qrows, :LAT] = nn(nope[:, lanes], wuk[hd]).astype(BF)
            pairs = rope[:, pl.ds(pl.multiple_of(i * 2 * ROPE, 2 * ROPE), 2 * ROPE)]
            q[qrows, LAT:] = pairs[:, hh * ROPE:(hh + 1) * ROPE]
            live_grad = (gh[:, lanes].astype(F32) * live).astype(BF)
            gl[:, lanes] = live_grad
            glt[:, lanes] = nt(wuv[hd], live_grad).astype(BF)
        return 0

    lax.fori_loop(0, H // 2, project, 0)
    mx[...] = jnp.full_like(mx, -1e30)

    def scores(base, n, masked):
        keys = kall[pl.ds(base, n), :]
        kt[:, pl.ds(base, n)] = keys.T

        def one(i, _):
            cols = pl.ds(pl.multiple_of(i * PAIR, PAIR), PAIR)
            sv = nt(kall[pl.ds(base, n), :], q[cols, :])
            if masked:
                j = lax.broadcasted_iota(jnp.int32, (n, PAIR), 0)
                t = lax.broadcasted_iota(jnp.int32, (n, PAIR), 1) % T
                lim = jnp.where(j < GROUP, v0, GROUP + v1)
                low = jnp.where(t < GROUP, 0, GROUP)
                sv = jnp.where((j <= t) & (j >= low) & (j < lim), sv, -1e30)
            s[pl.ds(base, n), cols] = sv
            mx[:, cols] = jnp.maximum(mx[:, cols], jnp.max(sv.reshape(n // 8, 8, PAIR), axis=0))
            gp[pl.ds(base, n), cols] = nn(kall[pl.ds(base, n), :LAT], glt[:, cols])
            return 0

        lax.fori_loop(0, R // PAIR, one, 0)

    arrived(rows(y, ozh, c, par), rz.at[0])
    for k in (1, 3, 2):
        y_send(1, k).start()
    x_send(1, 0).start()
    c_send(1, 0, 0).start()
    scores(KP, T, True)
    for k in (1, 3, 2):
        y_wait(0, 4 - k)
        x_send(0, k).start()
        c_send(0, k, 0).start()
    for k in (1, 3, 2):
        y_wait(1, 4 - k)
        x_send(1, k).start()
        c_send(1, k, 0).start()
    x_wait(1, 0)
    c_send(1, 0, 1).start()
    for k in (1, 3, 2):
        x_wait(0, k)
        c_send(0, k, 1).start()
    for k in (1, 3, 2):
        x_wait(1, k)
        c_send(1, k, 1).start()
    for k in (0, 1, 3, 2):
        for zr_ in range(2):
            c_wait(zr_, k, 0)
            c_wait(zr_, k, 1)
        scores(pl.multiple_of(yk(k) * 4 * SH, 128), 4 * SH, False)

    def wv_copy(i):
        return rc(wvs.at[i], wvc.at[i], swv.at[i], rwv.at[i], sib)

    def wk_copy(i):
        return rc(wks.at[i], wkc.at[i], swk.at[i], rwk.at[i], sib)

    STEP = 128

    def softmax(i, _):
        cols = pl.ds(pl.multiple_of(i * PAIR, PAIR), PAIR)
        top = jnp.max(mx[:, cols], axis=0, keepdims=True)

        def expo(j, acc):
            rws = pl.ds(pl.multiple_of(j * STEP, STEP), STEP)
            e = jnp.exp((s[rws, cols] - top) * SCALE)
            s[rws, cols] = e
            return acc + jnp.sum(e.reshape(STEP // 8, 8, PAIR), axis=0)

        total = lax.fori_loop(0, KA // STEP, expo, jnp.zeros((8, PAIR), F32))
        inv = 1.0 / jnp.sum(total, axis=0, keepdims=True)

        def norm(j, _):
            rws = pl.ds(pl.multiple_of(j * STEP, STEP), STEP)
            e = s[rws, cols] * inv
            s[rws, cols] = e
            p[rws, cols] = e.astype(BF)
            return 0

        lax.fori_loop(0, KA // STEP, norm, 0)
        lot = nn(kt[:LAT, :], p[:, cols]).astype(BF)
        delta = jnp.sum(glt[:, cols].astype(F32) * lot.astype(F32), axis=0, keepdims=True)

        def grad(j, _):
            rws = pl.ds(pl.multiple_of(j * STEP, STEP), STEP)
            ds[rws, cols] = (s[rws, cols] * (gp[rws, cols] - delta) * SCALE).astype(BF)
            return 0

        lax.fori_loop(0, KA // STEP, grad, 0)
        for hh in range(2):
            lanes = pl.ds(pl.multiple_of((2 * i + hh) * T, T), T)
            wvt[...] = nn(lot[:, hh * T:(hh + 1) * T], gl[:, lanes]).reshape(8, 2, 32, VD)
            wvs[i, :, hh] = wvt[:, oc].reshape(4, 2, 32, VD).astype(BF)
            wvacc[i, :, hh] = wvt[:, c].reshape(4, 2, 32, VD)
        wv_copy(i).start()
        return 0

    lax.fori_loop(0, R // PAIR, softmax, 0)

    def key_grad(base, n):
        rws = pl.ds(base, n)
        g[rws, :] = nn(ds[rws, :], q[...])
        g[rws, :LAT] = g[rws, :LAT] + nt(p[rws, :], glt[...])

    def owner_head(o):
        return (o // 2) * 4 + 1 + o % 2

    key_grad(KP, T)
    as_[...] = g[KP:KA, :].reshape(8, 16, W).astype(BF)
    for o in range(8):
        cp = rc(as_.at[o], ar.at[h], sa1.at[o], ra1.at[h], {"head": owner_head(o), "ans": a})

        @pl.when(h != owner_head(o))
        def _():
            cp.start()

    def gc_copy(i):
        return rc(gs.at[pl.ds(2 * i, 2)], gcr.at[pl.ds(2 * i, 2)], sgc.at[i], rgc.at[i], sib)

    def prompt_grad(i, _):
        base = pl.multiple_of(i * 4 * SH, 128)
        key_grad(base, 4 * SH)
        for zz in range(2):
            gs[2 * i + zz] = g[pl.ds(pl.multiple_of(base + zz * 192 + oc * SH, 8), SH), :].astype(BF)
        gc_copy(i).start()
        return 0

    lax.fori_loop(0, 4, prompt_grad, 0)

    def flip(i, m1, m3):
        odd = i % 2
        return m1 * (1 - odd) + m3 * odd, m3 * (1 - odd) + m1 * odd

    def y_first(i, buf, rbuf, ssem, rsem):
        pa, _ = flip(i, y1, y3)
        d = dev(x, pa, zh, zl, c)
        return (rc(buf.at[i, pa], rbuf.at[i, 0], ssem.at[4 + i], rsem.at[4 + i], d),
                rc(buf.at[i, (y + 2) % 4], rbuf.at[i, 1], ssem.at[8 + i], rsem.at[8 + i], d))

    def y_second(i, buf, rbuf, ssem, rsem):
        _, pb = flip(i, y1, y3)
        return rc(buf.at[i], rbuf.at[i], ssem.at[12 + i], rsem.at[12 + i], dev(x, pb, zh, zl, c))

    def z_hop(i, buf, rbuf, ssem, rsem):
        return rc(buf.at[i], rbuf.at[i], ssem.at[16 + i], rsem.at[16 + i], dev(x, y, ozh, zl, c))

    def wv_pair(i, _):
        wv_copy(i).wait_recv()
        t = wvacc[i] + wvc[i].astype(F32)
        wvacc[i] = t
        wvy[i] = t.astype(BF)
        for cp in y_first(i, wvy, wv1, swv, rwv):
            cp.start()
        return 0

    lax.fori_loop(0, 4, wv_pair, 0)

    def x_first(i):
        pa, _ = flip(i, x1, x3)
        d = dev(pa, y, zh, zl, c)
        return (rc(xs.at[i, pa], xr1.at[i, 0], sx1.at[i], rx1.at[i], d),
                rc(xs.at[i, (x + 2) % 4], xr1.at[i, 1], sx1.at[4 + i], rx1.at[4 + i], d))

    def x_second(i):
        _, pb = flip(i, x1, x3)
        return rc(xs2.at[i], xr2.at[i], sx2.at[i], rx2.at[i], dev(pb, y, zh, zl, c))

    def queries(i, _):
        gc_copy(i).wait_recv()
        for zz in range(2):
            base = pl.multiple_of(i * 4 * SH + zz * 192 + c * SH, 8)
            t = g[pl.ds(base, SH), :] + gcr[2 * i + zz].astype(F32)
            for half in range(2):
                piece = t[half * 48:(half + 1) * 48]
                xacc[i, 2 * zz + half] = piece
                xs[i, 2 * zz + half] = piece.astype(BF)
        for cp in x_first(i):
            cp.start()

        cols = pl.ds(pl.multiple_of(i * PAIR, PAIR), PAIR)
        gqt = nn(kt[...], ds[:, cols])
        glq = gqt[:LAT].astype(BF)
        rot = gqt[LAT:].T
        for hh in range(2):
            hd = 2 * i + hh
            lanes = pl.ds(pl.multiple_of(hd * T, T), T)
            part = glq[:, hh * T:(hh + 1) * T]
            o_nope[:, lanes] = nn(wuk[hd], part).T.astype(BF)
            nope_t = nope[:, lanes].astype(F32).T.astype(BF)
            wkt[...] = nt(nope_t, part).reshape(8, 2, 8, LAT)
            wks[i, :, hh] = wkt[:, oc].reshape(4, 16, LAT).astype(BF)
            wkacc[i, :, hh] = wkt[:, c].reshape(4, 16, LAT)
        o_rope[:, pl.ds(pl.multiple_of(i * T, T), T)] = jnp.concatenate(
            [rot[:T], rot[T:]], axis=1).astype(BF)
        wk_copy(i).start()
        return 0

    lax.fori_loop(0, 4, queries, 0)

    def x_mid(i, _):
        first, second = x_first(i)
        _, pb = flip(i, x1, x3)
        first.wait_recv()
        second.wait_recv()
        xs2[i] = (xacc[i, pb] + xr1[i, 1].astype(F32)).astype(BF)
        x_second(i).start()
        ysum[i] = xacc[i, x] + xr1[i, 0].astype(F32)
        return 0

    lax.fori_loop(0, 4, x_mid, 0)

    def wk_pair(i, _):
        wk_copy(i).wait_recv()
        t = wkacc[i] + wkc[i].astype(F32)
        wkacc[i] = t
        wky[i] = t.astype(BF)
        for cp in y_first(i, wky, wk1, swk, rwk):
            cp.start()
        return 0

    lax.fori_loop(0, 4, wk_pair, 0)

    is_owner = (zl == 1) | (zl == 2)
    mine = x * 2 + zl - 1

    def answer_out(i):
        return rc(fa, aa.at[mine], sa2.at[i - 1], ra2.at[mine], {"head": (h + i) % 16, "ans": a})

    @pl.when(is_owner)
    def _():
        ar[h] = as_[mine]
        acc = jnp.zeros((16, W), F32)
        for i in range(1, 16):
            src = (h + i) % 16
            arrived(ar.at[src], ra1.at[src])
        for i in range(16):
            acc = acc + ar[i].astype(F32)
        fa[...] = acc.astype(BF)
        for i in range(1, 16):
            answer_out(i).start()
        aa[mine] = fa[...]

    def wv_mid(i, _):
        first, second = y_first(i, wvy, wv1, swv, rwv)
        _, pb = flip(i, y1, y3)
        first.wait_recv()
        second.wait_recv()
        wv2s[i] = (wvacc[i, pb] + wv1[i, 1].astype(F32)).astype(BF)
        y_second(i, wv2s, wv2r, swv, rwv).start()
        wvz[i] = wvacc[i, y] + wv1[i, 0].astype(F32)
        return 0

    lax.fori_loop(0, 4, wv_mid, 0)

    def yy_copy(k):
        return rc(ys.at[yk(k)], yr.at[k - 1], syy.at[k - 1], ryy.at[k - 1], dev(x, yk(k), zh, zl, c))

    def x_last(i, _):
        x_second(i).wait_recv()
        t = ysum[i] + xr2[i].astype(F32)
        ysum[i] = t
        ys[i] = t.astype(BF)
        return 0

    lax.fori_loop(0, 4, x_last, 0)
    for k in (1, 3, 2):
        yy_copy(k).start()

    def wk_mid(i, _):
        first, second = y_first(i, wky, wk1, swk, rwk)
        _, pb = flip(i, y1, y3)
        first.wait_recv()
        second.wait_recv()
        wk2s[i] = (wkacc[i, pb] + wk1[i, 1].astype(F32)).astype(BF)
        y_second(i, wk2s, wk2r, swk, rwk).start()
        wkz[i] = (wkacc[i, y] + wk1[i, 0].astype(F32)).reshape(2, 2, 8, LAT)
        return 0

    lax.fori_loop(0, 4, wk_mid, 0)

    def wv_last(i, _):
        y_second(i, wv2s, wv2r, swv, rwv).wait_recv()
        wvz[i] = wvz[i] + wv2r[i].astype(F32)
        wvzs[i] = wvz[i, :, ozh].astype(BF)
        z_hop(i, wvzs, wvzr, swv, rwv).start()
        return 0

    lax.fori_loop(0, 4, wv_last, 0)

    acc = ysum[y]
    for k in (1, 3, 2):
        yy_copy(k).wait_recv()
    for k in (1, 3, 2):
        acc = acc + yr[k - 1].astype(F32)
    zs[...] = acc.reshape(3, 16, W).astype(BF)
    goal = x // 2
    me_z = zh * 4 + zl

    def zz_copy(i):
        return rc(zs.at[i], zr.at[me_z], szz.at[i], rzz.at[me_z], dev(x, y, goal, i, c))

    for i in range(3):
        @pl.when(me_z != goal * 4 + i)
        def _():
            zz_copy(i).start()

    def wk_last(i, _):
        y_second(i, wk2s, wk2r, swk, rwk).wait_recv()
        wkz[i] = wkz[i] + wk2r[i].astype(F32).reshape(2, 2, 8, LAT)
        wkzs[i] = wkz[i, :, ozh].reshape(16, LAT).astype(BF)
        z_hop(i, wkzs, wkzr, swk, rwk).start()
        return 0

    lax.fori_loop(0, 4, wk_last, 0)

    is_src = (zh == goal) & (zl < 3)
    piece = (x % 2) * 3 + zl

    def ag_copy(i):
        return rc(fz, ag.at[piece], sag.at[i - 1], rag.at[piece], {"head": (h + i) % 16, "ans": a})

    @pl.when(is_src)
    def _():
        zr[me_z] = zs[zl]
        for i in range(1, 8):
            src = (me_z + i) % 8
            arrived(zr.at[src], rzz.at[src])
        tot = jnp.zeros((16, W), F32)
        for i in range(8):
            tot = tot + zr[i].astype(F32)
        fz[...] = tot.astype(BF)
        for i in range(1, 16):
            ag_copy(i).start()
        ag[piece] = fz[...]

    for o in range(8):
        @pl.when(h != owner_head(o))
        def _():
            arrived(aa.at[o], ra2.at[o])

    o_ans[...] = aa[...].astype(F32).reshape(T, W)

    def weights_out(i, _):
        z_hop(i, wvzs, wvzr, swv, rwv).wait_recv()
        o_wv[pl.ds(2 * i, 2)] = wvz[i, :, zh] + wvzr[i].astype(F32)
        z_hop(i, wkzs, wkzr, swk, rwk).wait_recv()
        o_wk[pl.ds(2 * i, 2)] = wkz[i, :, zh] + wkzr[i].astype(F32).reshape(2, 8, LAT)
        return 0

    lax.fori_loop(0, 4, weights_out, 0)

    for i in range(6):
        @pl.when(h != (2 * zh + i // 3) * 4 + i % 3)
        def _():
            arrived(ag.at[i], rag.at[i])

    o_prm[...] = ag[...].astype(F32).reshape(SH, W)

    for zr_ in range(2):
        for k in (1, 2, 3):
            y_send(zr_, k).wait_send()
        for k in range(4):
            if zr_ + k > 0:
                x_send(zr_, k).wait_send()
            for second in range(2):
                c_send(zr_, k, second).wait_send()

    @pl.when((zl == 3) | (zl == 0))
    def _():
        sent(own_half, sz.at[0])
        sent(own_half, sz.at[1])

    for o in range(8):
        @pl.when(h != owner_head(o))
        def _():
            sent(as_.at[o], sa1.at[o])

    @pl.when(is_owner)
    def _():
        for i in range(1, 16):
            sent(fa, sa2.at[i - 1])

    @pl.when(is_src)
    def _():
        for i in range(1, 16):
            sent(fz, sag.at[i - 1])

    for i in range(3):
        @pl.when(me_z != goal * 4 + i)
        def _():
            sent(zs.at[i], szz.at[i])

    for k in (1, 2, 3):
        yy_copy(k).wait_send()

    def drain(i, _):
        gc_copy(i).wait_send()
        wv_copy(i).wait_send()
        wk_copy(i).wait_send()
        for cp in x_first(i):
            cp.wait_send()
        x_second(i).wait_send()
        for cp in y_first(i, wvy, wv1, swv, rwv) + y_first(i, wky, wk1, swk, rwk):
            cp.wait_send()
        y_second(i, wv2s, wv2r, swv, rwv).wait_send()
        y_second(i, wk2s, wk2r, swk, rwk).wait_send()
        z_hop(i, wvzs, wvzr, swv, rwv).wait_send()
        z_hop(i, wkzs, wkzr, swk, rwk).wait_send()
        return 0

    lax.fori_loop(0, 4, drain, 0)


def per_device(*args):
    V = pltpu.VMEM
    D = pltpu.SemaphoreType.DMA
    scratch = [
        V((KA, W), BF), V((W, KA), BF), V((R, W), BF), V((LAT, R), BF), V((T, H * VD), BF),
        V((KA, R), F32), V((KA, R), F32), V((KA, R), BF), V((KA, R), BF), V((8, R), F32), V((KA, W), F32),
        V((8, SH, W), BF), V((8, SH, W), BF), V((4, 4, 48, W), BF), V((4, 4, 48, W), F32),
        V((4, 2, 48, W), BF), V((4, 48, W), BF), V((4, 48, W), BF), V((4, 48, W), F32),
        V((4, 48, W), BF), V((3, 48, W), BF), V((3, 16, W), BF), V((8, 16, W), BF),
        V((16, W), BF), V((6, 16, W), BF),
        V((8, 16, W), BF), V((16, 16, W), BF), V((16, W), BF), V((8, 16, W), BF),
        V((8, 2, 32, VD), F32), V((4, 4, 2, 2, 32, VD), BF), V((4, 4, 2, 2, 32, VD), BF),
        V((4, 4, 2, 2, 32, VD), F32), V((4, 4, 2, 2, 32, VD), BF), V((4, 2, 2, 2, 32, VD), BF),
        V((4, 2, 2, 32, VD), BF), V((4, 2, 2, 32, VD), BF), V((4, 2, 2, 32, VD), F32),
        V((4, 2, 32, VD), BF), V((4, 2, 32, VD), BF),
        V((8, 2, 8, LAT), F32), V((4, 4, 2, 16, LAT), BF), V((4, 4, 2, 16, LAT), BF),
        V((4, 4, 2, 16, LAT), F32), V((4, 4, 2, 16, LAT), BF), V((4, 2, 2, 16, LAT), BF),
        V((4, 2, 16, LAT), BF), V((4, 2, 16, LAT), BF), V((4, 2, 2, 8, LAT), F32),
        V((4, 16, LAT), BF), V((4, 16, LAT), BF),
        D((6,)), D((6,)), D((3,)), D((1,)), D((8,)), D((8,)), D((16,)), D((16,)),
        D((4,)), D((4,)), D((8,)), D((8,)), D((4,)), D((4,)), D((3,)), D((3,)), D((3,)), D((8,)), D((15,)), D((6,)),
        D((8,)), D((16,)), D((15,)), D((8,)),
        D((20,)), D((20,)), D((20,)), D((20,)),
    ]
    vm = pl.BlockSpec(memory_space=pltpu.VMEM)
    return pl.pallas_call(
        kernel,
        out_shape=(
            jax.ShapeDtypeStruct((T, H * HD), BF),
            jax.ShapeDtypeStruct((T, H * ROPE), BF),
            jax.ShapeDtypeStruct((T, W), F32),
            jax.ShapeDtypeStruct((SH, W), F32),
            jax.ShapeDtypeStruct((H, 8, LAT), F32),
            jax.ShapeDtypeStruct((H, 32, VD), F32),
        ),
        in_specs=[vm] * 7 + [pl.BlockSpec(memory_space=pltpu.SMEM)],
        out_specs=(vm,) * 6,
        scratch_shapes=scratch,
        compiler_params=pltpu.CompilerParams(
            collective_id=0, has_side_effects=True, vmem_limit_bytes=62 * 1024 * 1024
        ),
    )(*args)


def solution(mesh):
    return jax.shard_map(
        per_device,
        mesh=mesh,
        in_specs=(
            P("ans", "head"),
            P("ans", "head"),
            P("ans", None),
            P("ans", None),
            P("head", None, None),
            P("head", None, None),
            P("ans", "head"),
            P("ans"),
        ),
        out_specs=(
            P("ans", "head"),
            P("ans", "head"),
            P("ans", None),
            P("ans", None),
            P("head", "ans", None),
            P("head", "ans", None),
        ),
        check_vma=False,
    )
```

```python
import jax
import jax.numpy as jnp
from jax import lax
from jax.experimental import pallas as pl
from jax.experimental.pallas import tpu as pltpu
from jax.sharding import PartitionSpec as P

LAT = 512
ROPE = 64
HD = 128
VD = 128
GROUP = 64
W = LAT + ROPE
MESH = pl.DeviceIdType.MESH
F32 = jnp.float32
BF = jnp.bfloat16
SCALE = (HD + ROPE) ** (-0.5)

T = 128
H = 8
R = T * H
SH = 96
KP = 1536
KA = KP + T
PAIR = 2 * T


def nn(a, b):
    return jnp.dot(a, b, preferred_element_type=F32)


def nt(a, b):
    return lax.dot_general(a, b, (((1,), (1,)), ((), ())), preferred_element_type=F32)


def kernel(
    nope_in, rope_in, ans_in, prm_in, wuk_in, wuv_in, gh_in, valid,
    o_nope, o_rope, o_ans, o_prm, o_wk, o_wv,
    nope, rope, wuk, wuv, gh, v_nope, v_rope, v_ans, v_prm, v_wk, v_wv,
    kall, kt, q, glt, gl, s, gp, p, ds, mx, g,
    gs, gcr, xs, xr, zacc, zs, zr, fz, ag,
    as_, ar, fa, aa,
    wvt, wvs, wvc, wvacc, wvy, wvr, wvz, wvzs, wvzr,
    wkt, wks, wkc, wkacc, wky, wkr, wkz, wkzs, wkzr,
    sin, sout,
    sy, ry, sz, rz, sx, rx, scc, rcc,
    sgc, rgc, sxy, rxy, szz, rzz, sag, rag,
    sa1, ra1, sa2, ra2,
    swv, rwv, swk, rwk,
):
    h = lax.axis_index("head")
    a = lax.axis_index("ans")
    x, zl = h // 4, h % 4
    y, zh, c = a // 4, (a // 2) % 2, a % 2
    oc, ozh = 1 - c, 1 - zh
    par = x % 2

    def dev(x_, y_, zh_, zl_, c_):
        return {"head": x_ * 4 + zl_, "ans": y_ * 4 + zh_ * 2 + c_}

    sib = dev(x, y, zh, zl, oc)

    def rc(src, dst, ss, rs, d):
        return pltpu.make_async_remote_copy(
            src_ref=src, dst_ref=dst, send_sem=ss, recv_sem=rs, device_id=d, device_id_type=MESH
        )

    def arrived(dst, rs):
        rc(dst, dst, rs, rs, sib).wait_recv()

    def sent(src, ss):
        rc(src, src, ss, ss, sib).wait_send()

    def yk(k):
        return (y + k) % 4

    partners = [dev((x + i) % 4, (y + j) % 4, zh, zl, c) for i in range(4) for j in range(4) if i + j > 0]
    partners += [dev((x + i) % 4, y, zh, (zl + j) % 4, c) for i in range(4) for j in range(1, 4)]
    partners += [dev(x, y, ozh, i, c) for i in range(4)] + [sib]
    bar = pltpu.get_barrier_semaphore()
    for d in partners:
        pl.semaphore_signal(bar, inc=1, device_id=d, device_id_type=MESH)

    def rows(y_, zh_, c_, half=None):
        base = zh_ * 768 + y_ * 192 + c_ * SH
        if half is None:
            return kall.at[pl.ds(pl.multiple_of(base, 16), SH)]
        return kall.at[pl.ds(pl.multiple_of(base + half * 48, 16), 48)]

    loads = [
        pltpu.make_async_copy(src, dst, sin.at[i])
        for i, (src, dst) in enumerate(
            [(prm_in, rows(y, zh, c)), (nope_in, nope), (rope_in, rope), (wuk_in, wuk), (wuv_in, wuv),
             (gh_in, gh), (ans_in, kt.at[:, pl.ds(KP, T)])]
        )
    ]
    for cp in loads:
        cp.start()
    for cp in loads:
        cp.wait()

    v0, v1 = valid[0], valid[1]
    tok = lax.broadcasted_iota(jnp.int32, (T, T), 0)
    live = (tok % GROUP < jnp.where(tok < GROUP, v0, v1)).astype(F32)

    def project(i, _):
        for hh in range(2):
            hd = 2 * i + hh
            lanes = pl.ds(pl.multiple_of(hd * T, T), T)
            qrows = pl.ds(pl.multiple_of(hd * T, T), T)
            q[qrows, :LAT] = nn(nope[:, lanes], wuk[hd]).astype(BF)
            pairs = rope[:, pl.ds(pl.multiple_of(i * 2 * ROPE, 2 * ROPE), 2 * ROPE)]
            q[qrows, LAT:] = pairs[:, hh * ROPE:(hh + 1) * ROPE]
            live_grad = (gh[:, lanes].astype(F32) * live).astype(BF)
            gl[:, lanes] = live_grad
            glt[:, lanes] = nt(wuv[hd], live_grad).astype(BF)
        return 0

    lax.fori_loop(0, H // 2, project, 0, unroll=True)
    pl.semaphore_wait(bar, len(partners))

    own_half = rows(y, zh, c, par)

    def y_send(zr_, k):
        zz = zh if zr_ == 0 else ozh
        view = rows(y, zz, c, par)
        return rc(view, view, sy.at[zr_ * 3 + k - 1], ry.at[zr_ * 3 + k - 1], dev(x, yk(k), zh, zl, c))

    def y_wait(zr_, k):
        zz = zh if zr_ == 0 else ozh
        arrived(rows((y + 4 - k) % 4, zz, c, par), ry.at[zr_ * 3 + k - 1])

    def x_send(zr_, k):
        yy = yk(k)
        zz = zh if zr_ == 0 else ozh
        xt = (x + 1 + 2 * (yy % 2)) % 4
        view = rows(yy, zz, c, par)
        return rc(view, view, sx.at[zr_ * 4 + k], rx.at[zr_ * 4 + k], dev(xt, y, zh, zl, c))

    def x_wait(zr_, k):
        zz = zh if zr_ == 0 else ozh
        arrived(rows(yk(k), zz, c, 1 - par), rx.at[zr_ * 4 + k])

    def c_send(zr_, k, second):
        zz = zh if zr_ == 0 else ozh
        half = (1 - par) if second else par
        view = rows(yk(k), zz, c, half)
        i = (zr_ * 4 + k) * 2 + second
        return rc(view, view, scc.at[i], rcc.at[i], sib)

    def c_wait(zr_, k, second):
        zz = zh if zr_ == 0 else ozh
        half = (1 - par) if second else par
        i = (zr_ * 4 + k) * 2 + second
        arrived(rows(yk(k), zz, oc, half), rcc.at[i])

    def z_copy(to_zl, i):
        return rc(own_half, own_half, sz.at[i], rz.at[0], dev(x, y, ozh, to_zl, c))

    @pl.when(zl == 3)
    def _():
        z_copy(1, 1).start()
        z_copy(0, 0).start()

    @pl.when(zl == 0)
    def _():
        z_copy(2, 1).start()
        z_copy(3, 0).start()

    for k in (2, 1, 3):
        y_send(0, k).start()
    c_send(0, 0, 0).start()
    c_send(0, 0, 1).start()

    mx[...] = jnp.full_like(mx, -1e30)

    def scores(base, n, masked):
        def one(i, _):
            cols = pl.ds(pl.multiple_of(i * PAIR, PAIR), PAIR)
            sv = nt(kall[pl.ds(base, n), :], q[cols, :])
            if masked:
                j = lax.broadcasted_iota(jnp.int32, (n, PAIR), 0)
                t = lax.broadcasted_iota(jnp.int32, (n, PAIR), 1) % T
                lim = jnp.where(j < GROUP, v0, GROUP + v1)
                low = jnp.where(t < GROUP, 0, GROUP)
                sv = jnp.where((j <= t) & (j >= low) & (j < lim), sv, -1e30)
            s[pl.ds(base, n), cols] = sv
            mx[:, cols] = jnp.maximum(mx[:, cols], jnp.max(sv.reshape(n // 8, 8, PAIR), axis=0))
            gp[pl.ds(base, n), cols] = nn(kall[pl.ds(base, n), :LAT], glt[:, cols])
            return 0

        lax.fori_loop(0, R // PAIR, one, 0, unroll=True)

    def prompt_scores(base):
        base = pl.multiple_of(base, 128)
        kt[:, pl.ds(base, 384)] = kall[pl.ds(base, 384), :].T
        scores(base, 384, False)

    kall[KP:KA, :] = kt[:, KP:KA].T
    scores(KP, T, True)
    arrived(rows(y, ozh, c, par), rz.at[0])
    for k in (2, 1, 3):
        y_send(1, k).start()
    x_send(1, 0).start()
    c_send(1, 0, 0).start()
    for k in (1, 3, 2):
        y_wait(0, 4 - k)
        x_send(0, k).start()
        c_send(0, k, 0).start()
    for k in (1, 3, 2):
        x_wait(0, k)
        c_send(0, k, 1).start()
    for k in range(4):
        for second in range(2):
            c_wait(0, k, second)
    prompt_scores(zh * 768)
    for k in (1, 3, 2):
        y_wait(1, 4 - k)
        x_send(1, k).start()
        c_send(1, k, 0).start()
    x_wait(1, 0)
    c_send(1, 0, 1).start()
    prompt_scores(zh * 768 + 384)
    for k in (1, 3, 2):
        x_wait(1, k)
        c_send(1, k, 1).start()
    for k in range(4):
        for second in range(2):
            c_wait(1, k, second)
    prompt_scores(ozh * 768)
    prompt_scores(ozh * 768 + 384)

    def wv_copy(i):
        return rc(wvs.at[i], wvc.at[i], swv.at[i], rwv.at[i], sib)

    def wk_copy(i):
        return rc(wks.at[i], wkc.at[i], swk.at[i], rwk.at[i], sib)

    def y_hop(i, k, buf, rbuf, ssem, rsem):
        n = 4 + 3 * i + k - 1
        return rc(buf.at[i, yk(k)], rbuf.at[i, k - 1], ssem.at[n], rsem.at[n], dev(x, yk(k), zh, zl, c))

    def z_hop(i, buf, rbuf, ssem, rsem):
        return rc(buf.at[i], rbuf.at[i], ssem.at[16 + i], rsem.at[16 + i], dev(x, y, ozh, zl, c))

    def wv_pair(i):
        wv_copy(i).wait_recv()
        t = wvacc[i] + wvc[i].astype(F32)
        wvacc[i] = t
        wvy[i] = t.astype(BF)
        for k in (2, 1, 3):
            y_hop(i, k, wvy, wvr, swv, rwv).start()

    def wk_pair(i):
        wk_copy(i).wait_recv()
        t = wkacc[i] + wkc[i].astype(F32)
        wkacc[i] = t
        wky[i] = t.astype(BF)
        for k in (2, 1, 3):
            y_hop(i, k, wky, wkr, swk, rwk).start()

    STEP = 128

    def softmax(i, _):
        cols = pl.ds(pl.multiple_of(i * PAIR, PAIR), PAIR)
        top = jnp.max(mx[:, cols], axis=0, keepdims=True)

        def expo(j, acc):
            rws = pl.ds(pl.multiple_of(j * STEP, STEP), STEP)
            e = jnp.exp((s[rws, cols] - top) * SCALE)
            s[rws, cols] = e
            return acc + jnp.sum(e.reshape(STEP // 8, 8, PAIR), axis=0)

        total = lax.fori_loop(0, KA // STEP, expo, jnp.zeros((8, PAIR), F32), unroll=True)
        inv = 1.0 / jnp.sum(total, axis=0, keepdims=True)

        def norm(j, _):
            rws = pl.ds(pl.multiple_of(j * STEP, STEP), STEP)
            e = s[rws, cols] * inv
            s[rws, cols] = e
            p[rws, cols] = e.astype(BF)
            return 0

        lax.fori_loop(0, KA // STEP, norm, 0, unroll=True)
        lot = nn(kt[:LAT, :], p[:, cols]).astype(BF)
        delta = jnp.sum(glt[:, cols].astype(F32) * lot.astype(F32), axis=0, keepdims=True)

        def grad(j, _):
            rws = pl.ds(pl.multiple_of(j * STEP, STEP), STEP)
            ds[rws, cols] = (s[rws, cols] * (gp[rws, cols] - delta) * SCALE).astype(BF)
            return 0

        lax.fori_loop(0, KA // STEP, grad, 0, unroll=True)
        for hh in range(2):
            lanes = pl.ds(pl.multiple_of((2 * i + hh) * T, T), T)
            wvt[...] = nn(lot[:, hh * T:(hh + 1) * T], gl[:, lanes]).reshape(8, 2, 32, VD)
            wvs[i, :, hh] = wvt[:, oc].reshape(4, 2, 32, VD).astype(BF)
            wvacc[i, :, hh] = wvt[:, c].reshape(4, 2, 32, VD)
        wv_copy(i).start()

        @pl.when(i > 0)
        def _():
            wv_pair(i - 1)

        return 0

    lax.fori_loop(0, R // PAIR, softmax, 0)

    def key_grad(base, n):
        rws = pl.ds(base, n)
        g[rws, :] = nn(ds[rws, :], q[...])
        g[rws, :LAT] = g[rws, :LAT] + nt(p[rws, :], glt[...])

    def owner_head(o):
        return (o // 2) * 4 + 1 + o % 2

    key_grad(KP, T)
    wv_pair(3)
    as_[...] = g[KP:KA, :].reshape(8, 16, W).astype(BF)
    for o in range(8):
        cp = rc(as_.at[o], ar.at[h], sa1.at[o], ra1.at[h], {"head": owner_head(o), "ans": a})

        @pl.when(h != owner_head(o))
        def _():
            cp.start()

    def gc_copy(i):
        return rc(gs.at[pl.ds(2 * i, 2)], gcr.at[pl.ds(2 * i, 2)], sgc.at[i], rgc.at[i], sib)

    def xy_copy(yy, xx):
        n = yy * 4 + xx
        m = y * 4 + x
        return rc(xs.at[n], xr.at[m], sxy.at[n], rxy.at[m], dev(xx, yy, zh, zl, c))

    def to_owner(i):
        gc_copy(i).wait_recv()
        for b in range(2):
            base = pl.multiple_of(i * 384 + b * 192 + c * SH, 8)
            t = g[pl.ds(base, SH), :] + gcr[2 * i + b].astype(F32)
            yy = 2 * (i % 2) + b
            for half in range(2):
                xx = 2 * (i // 2) + half
                part = t[half * 48:(half + 1) * 48]
                xs[yy * 4 + xx] = part.astype(BF)
                mine = (yy == y) & (xx == x)

                @pl.when(mine)
                def _():
                    zacc[...] = part

                @pl.when(jnp.logical_not(mine))
                def _():
                    xy_copy(yy, xx).start()

    def prompt_grad(i):
        base = i * 384
        key_grad(base, 384)
        for b in range(2):
            gs[2 * i + b] = g[pl.ds(pl.multiple_of(base + b * 192 + oc * SH, 8), SH), :].astype(BF)
        gc_copy(i).start()
        if i > 0:
            to_owner(i - 1)

    for i in range(4):
        prompt_grad(i)
    to_owner(3)

    def queries(i, _):
        cols = pl.ds(pl.multiple_of(i * PAIR, PAIR), PAIR)
        gqt = nn(kt[...], ds[:, cols])
        glq = gqt[:LAT].astype(BF)
        rot = gqt[LAT:].T
        for hh in range(2):
            hd = 2 * i + hh
            lanes = pl.ds(pl.multiple_of(hd * T, T), T)
            part = glq[:, hh * T:(hh + 1) * T]
            v_nope[:, lanes] = nn(wuk[hd], part).T.astype(BF)
            nope_t = nope[:, lanes].astype(F32).T.astype(BF)
            wkt[...] = nt(nope_t, part).reshape(8, 2, 8, LAT)
            wks[i, :, hh] = wkt[:, oc].reshape(4, 16, LAT).astype(BF)
            wkacc[i, :, hh] = wkt[:, c].reshape(4, 16, LAT)
        v_rope[:, pl.ds(pl.multiple_of(i * T, T), T)] = jnp.concatenate(
            [rot[:T], rot[T:]], axis=1).astype(BF)
        wk_copy(i).start()

        @pl.when(i > 0)
        def _():
            wk_pair(i - 1)

        return 0

    lax.fori_loop(0, 4, queries, 0)
    out_nope = pltpu.make_async_copy(v_nope, o_nope, sout.at[0])
    out_rope = pltpu.make_async_copy(v_rope, o_rope, sout.at[1])
    out_nope.start()
    out_rope.start()
    wk_pair(3)

    def wv_mid(i, _):
        for k in (1, 2, 3):
            y_hop(i, k, wvy, wvr, swv, rwv).wait_recv()
        t = wvacc[i, y]
        for k in (1, 2, 3):
            t = t + wvr[i, k - 1].astype(F32)
        wvz[i] = t
        wvzs[i] = wvz[i, :, ozh].astype(BF)
        z_hop(i, wvzs, wvzr, swv, rwv).start()
        return 0

    lax.fori_loop(0, 4, wv_mid, 0)

    is_owner = (zl == 1) | (zl == 2)
    mine = x * 2 + zl - 1

    def answer_out(i):
        return rc(fa, aa.at[mine], sa2.at[i - 1], ra2.at[mine], {"head": (h + i) % 16, "ans": a})

    @pl.when(is_owner)
    def _():
        ar[h] = as_[mine]
        for i in range(1, 16):
            src = (h + i) % 16
            arrived(ar.at[src], ra1.at[src])
        acc = jnp.zeros((16, W), F32)
        for i in range(16):
            acc = acc + ar[i].astype(F32)
        fa[...] = acc.astype(BF)
        for i in range(1, 16):
            answer_out(i).start()
        aa[mine] = fa[...]

    me_xy = y * 4 + x
    for i in range(1, 16):
        src = (me_xy + i) % 16
        arrived(xr.at[src], rxy.at[src])
    xr[me_xy] = jnp.zeros((48, W), BF)
    acc = zacc[...]
    for i in range(16):
        acc = acc + xr[i].astype(F32)
    zs[...] = acc.reshape(3, 16, W).astype(BF)
    goal = x // 2
    me_z = zh * 4 + zl

    def zz_copy(i):
        return rc(zs.at[i], zr.at[me_z], szz.at[i], rzz.at[me_z], dev(x, y, goal, i, c))

    for i in range(3):
        @pl.when(me_z != goal * 4 + i)
        def _():
            zz_copy(i).start()

    def wk_mid(i, _):
        for k in (1, 2, 3):
            y_hop(i, k, wky, wkr, swk, rwk).wait_recv()
        t = wkacc[i, y]
        for k in (1, 2, 3):
            t = t + wkr[i, k - 1].astype(F32)
        wkz[i] = t.reshape(2, 2, 8, LAT)
        wkzs[i] = wkz[i, :, ozh].reshape(16, LAT).astype(BF)
        z_hop(i, wkzs, wkzr, swk, rwk).start()
        return 0

    lax.fori_loop(0, 4, wk_mid, 0)

    is_src = (zh == goal) & (zl < 3)
    piece = (x % 2) * 3 + zl

    def ag_copy(i):
        return rc(fz, ag.at[piece], sag.at[i - 1], rag.at[piece], {"head": (h + i) % 16, "ans": a})

    @pl.when(is_src)
    def _():
        zr[me_z] = zs[zl]
        for i in range(1, 8):
            src = (me_z + i) % 8
            arrived(zr.at[src], rzz.at[src])
        tot = jnp.zeros((16, W), F32)
        for i in range(8):
            tot = tot + zr[i].astype(F32)
        fz[...] = tot.astype(BF)
        for i in range(1, 16):
            ag_copy(i).start()
        ag[piece] = fz[...]

    for o in range(8):
        @pl.when(h != owner_head(o))
        def _():
            arrived(aa.at[o], ra2.at[o])

    v_ans[...] = aa[...].astype(F32).reshape(T, W).T
    out_ans = pltpu.make_async_copy(v_ans, o_ans, sout.at[2])
    out_ans.start()

    def weights_out(i, _):
        z_hop(i, wvzs, wvzr, swv, rwv).wait_recv()
        v_wv[pl.ds(2 * i, 2)] = wvz[i, :, zh] + wvzr[i].astype(F32)
        z_hop(i, wkzs, wkzr, swk, rwk).wait_recv()
        v_wk[pl.ds(2 * i, 2)] = wkz[i, :, zh] + wkzr[i].astype(F32).reshape(2, 8, LAT)
        return 0

    lax.fori_loop(0, 4, weights_out, 0)
    out_wk = pltpu.make_async_copy(v_wk, o_wk, sout.at[3])
    out_wv = pltpu.make_async_copy(v_wv, o_wv, sout.at[4])
    out_wk.start()
    out_wv.start()

    for zr_ in range(2):
        for k in (1, 2, 3):
            y_send(zr_, k).wait_send()
        for k in range(4):
            if zr_ + k > 0:
                x_send(zr_, k).wait_send()
            for second in range(2):
                c_send(zr_, k, second).wait_send()

    @pl.when((zl == 3) | (zl == 0))
    def _():
        sent(own_half, sz.at[0])
        sent(own_half, sz.at[1])

    for o in range(8):
        @pl.when(h != owner_head(o))
        def _():
            sent(as_.at[o], sa1.at[o])

    @pl.when(is_owner)
    def _():
        for i in range(1, 16):
            sent(fa, sa2.at[i - 1])

    for i in range(3):
        @pl.when(me_z != goal * 4 + i)
        def _():
            sent(zs.at[i], szz.at[i])

    for i in range(1, 16):
        dst = (me_xy + i) % 16
        sent(xs.at[dst], sxy.at[dst])

    def drain(i, _):
        gc_copy(i).wait_send()
        wv_copy(i).wait_send()
        wk_copy(i).wait_send()
        for k in (1, 2, 3):
            y_hop(i, k, wvy, wvr, swv, rwv).wait_send()
            y_hop(i, k, wky, wkr, swk, rwk).wait_send()
        z_hop(i, wvzs, wvzr, swv, rwv).wait_send()
        z_hop(i, wkzs, wkzr, swk, rwk).wait_send()
        return 0

    lax.fori_loop(0, 4, drain, 0)

    for i in range(6):
        @pl.when(h != (2 * zh + i // 3) * 4 + i % 3)
        def _():
            arrived(ag.at[i], rag.at[i])

    v_prm[...] = ag[...].astype(F32).reshape(SH, W)
    out_prm = pltpu.make_async_copy(v_prm, o_prm, sout.at[5])
    out_prm.start()

    @pl.when(is_src)
    def _():
        for i in range(1, 16):
            sent(fz, sag.at[i - 1])

    for cp in (out_nope, out_rope, out_ans, out_wk, out_wv, out_prm):
        cp.wait()


def hand_over(*refs):
    for i in range(6):
        refs[6 + i][...] = refs[i][...]


def per_device(nope, rope, ans, *rest):
    V = pltpu.VMEM
    D = pltpu.SemaphoreType.DMA
    outs = (
        jax.ShapeDtypeStruct((T, H * HD), BF),
        jax.ShapeDtypeStruct((T, H * ROPE), BF),
        jax.ShapeDtypeStruct((W, T), F32),
        jax.ShapeDtypeStruct((SH, W), F32),
        jax.ShapeDtypeStruct((H, 8, LAT), F32),
        jax.ShapeDtypeStruct((H, 32, VD), F32),
    )
    scratch = [
        V((T, H * HD), BF), V((T, H * ROPE), BF), V((H, HD, LAT), BF), V((H, LAT, VD), BF), V((T, H * VD), BF),
    ] + [V(o.shape, o.dtype) for o in outs] + [
        V((KA, W), BF), V((W, KA), BF), V((R, W), BF), V((LAT, R), BF), V((T, H * VD), BF),
        V((KA, R), F32), V((KA, R), F32), V((KA, R), BF), V((KA, R), BF), V((8, R), F32), V((KA, W), F32),
        V((8, SH, W), BF), V((8, SH, W), BF), V((16, 48, W), BF), V((16, 48, W), BF), V((48, W), F32),
        V((3, 16, W), BF), V((8, 16, W), BF), V((16, W), BF), V((6, 16, W), BF),
        V((8, 16, W), BF), V((16, 16, W), BF), V((16, W), BF), V((8, 16, W), BF),
        V((8, 2, 32, VD), F32), V((4, 4, 2, 2, 32, VD), BF), V((4, 4, 2, 2, 32, VD), BF),
        V((4, 4, 2, 2, 32, VD), F32), V((4, 4, 2, 2, 32, VD), BF), V((4, 3, 2, 2, 32, VD), BF),
        V((4, 2, 2, 32, VD), F32), V((4, 2, 32, VD), BF), V((4, 2, 32, VD), BF),
        V((8, 2, 8, LAT), F32), V((4, 4, 2, 16, LAT), BF), V((4, 4, 2, 16, LAT), BF),
        V((4, 4, 2, 16, LAT), F32), V((4, 4, 2, 16, LAT), BF), V((4, 3, 2, 16, LAT), BF),
        V((4, 2, 2, 8, LAT), F32), V((4, 16, LAT), BF), V((4, 16, LAT), BF),
        D((7,)), D((6,)),
        D((6,)), D((6,)), D((2,)), D((1,)), D((8,)), D((8,)), D((16,)), D((16,)),
        D((4,)), D((4,)), D((16,)), D((16,)), D((3,)), D((8,)), D((15,)), D((6,)),
        D((8,)), D((16,)), D((15,)), D((8,)),
        D((20,)), D((20,)), D((20,)), D((20,)),
    ]
    hbm = pl.BlockSpec(memory_space=pl.ANY)
    got = pl.pallas_call(
        kernel,
        out_shape=outs,
        in_specs=[hbm] * 7 + [pl.BlockSpec(memory_space=pltpu.SMEM)],
        out_specs=(hbm,) * 6,
        scratch_shapes=scratch,
        compiler_params=pltpu.CompilerParams(
            collective_id=0, has_side_effects=True, vmem_limit_bytes=62 * 1024 * 1024
        ),
    )(nope, rope, ans.T, *rest)
    res = pl.pallas_call(
        hand_over,
        out_shape=outs,
        in_specs=[pl.BlockSpec(memory_space=pltpu.VMEM)] * 6,
        out_specs=(pl.BlockSpec(memory_space=pltpu.VMEM),) * 6,
    )(*got)
    return res[0], res[1], res[2].T, res[3], res[4], res[5]


def solution(mesh):
    return jax.shard_map(
        per_device,
        mesh=mesh,
        in_specs=(
            P("ans", "head"),
            P("ans", "head"),
            P("ans", None),
            P("ans", None),
            P("head", None, None),
            P("head", None, None),
            P("ans", "head"),
            P("ans"),
        ),
        out_specs=(
            P("ans", "head"),
            P("ans", "head"),
            P("ans", None),
            P("ans", None),
            P("head", "ans", None),
            P("head", "ans", None),
        ),
        check_vma=False,
    )
```

```python
import jax
import jax.numpy as jnp
from jax import lax
from jax.experimental import pallas as pl
from jax.experimental.pallas import tpu as pltpu
from jax.sharding import PartitionSpec as P

LAT = 512
ROPE = 64
HD = 128
VD = 128
GROUP = 64
W = LAT + ROPE
MESH = pl.DeviceIdType.MESH
F32 = jnp.float32
BF = jnp.bfloat16
SCALE = (HD + ROPE) ** (-0.5)
EXP2 = SCALE * 1.4426950408889634

T = 128
H = 8
R = T * H
SH = 96
KP = 1536
KA = KP + T
PAIR = 2 * T


def nn(a, b):
    return jnp.dot(a, b, preferred_element_type=F32)


def nt(a, b):
    return lax.dot_general(a, b, (((1,), (1,)), ((), ())), preferred_element_type=F32)


def kernel(
    nope_in, rope_in, ans_in, prm_in, wuk_in, wuv_in, gh_in, valid,
    o_nope, o_rope, o_ans, o_prm, o_wk, o_wv,
    nope, rope, wuk, wuv, gh, v_nope, v_rope, v_ans, v_prm, v_wk, v_wv,
    kall, kt, q, glt, glp, gl, s, gp, p, ds, mx, g,
    gs, gcr, xs, xr, zacc, zs, zr, fz, ag,
    as_, ar, fa, aa,
    wvt, wvs, wvc, wvacc, wvy, wvr, wvz, wvzs, wvzr,
    wkt, wks, wkc, wkacc, wky, wkr, wkz, wkzs, wkzr,
    sin, sout,
    sz, rz, sn, rn, sf, rf, scc, rcc,
    sgc, rgc, sxy, rxy, szz, rzz, sag, rag,
    sa1, ra1, sa2, ra2,
    swv, rwv, swk, rwk,
):
    h = lax.axis_index("head")
    a = lax.axis_index("ans")
    x, zl = h // 4, h % 4
    y, zh, c = a // 4, (a // 2) % 2, a % 2
    oc, ozh = 1 - c, 1 - zh
    hx = x % 2

    def dev(x_, y_, zh_, zl_, c_):
        return {"head": x_ * 4 + zl_, "ans": y_ * 4 + zh_ * 2 + c_}

    sib = dev(x, y, zh, zl, oc)

    def rc(src, dst, ss, rs, d):
        return pltpu.make_async_remote_copy(
            src_ref=src, dst_ref=dst, send_sem=ss, recv_sem=rs, device_id=d, device_id_type=MESH
        )

    def arrived(dst, rs):
        rc(dst, dst, rs, rs, sib).wait_recv()

    def sent(src, ss):
        rc(src, src, ss, ss, sib).wait_send()

    def yk(k):
        return (y + k) % 4

    partners = [dev((x + i) % 4, (y + j) % 4, zh, zl, c) for i in range(4) for j in range(4) if i + j > 0]
    partners += [dev((x + i) % 4, y, zh, (zl + j) % 4, c) for i in range(4) for j in range(1, 4)]
    partners += [dev(x, y, ozh, i, c) for i in range(4)] + [sib]
    bar = pltpu.get_barrier_semaphore()
    for d in partners:
        pl.semaphore_signal(bar, inc=1, device_id=d, device_id_type=MESH)

    def rows(y_, zh_, c_, half=None):
        base = zh_ * 768 + c_ * 384 + y_ * SH
        if half is None:
            return kall.at[pl.ds(pl.multiple_of(base, 16), SH)]
        return kall.at[pl.ds(pl.multiple_of(base + half * 48, 16), 48)]

    loads = [
        pltpu.make_async_copy(src, dst, sin.at[i])
        for i, (src, dst) in enumerate(
            [(prm_in, rows(y, zh, c)), (nope_in, nope), (rope_in, rope), (wuk_in, wuk), (wuv_in, wuv),
             (gh_in, gh), (ans_in, kt.at[:, pl.ds(KP, T)])]
        )
    ]
    for cp in loads:
        cp.start()
    for cp in loads:
        cp.wait()

    v0, v1 = valid[0], valid[1]
    tok = lax.broadcasted_iota(jnp.int32, (T, T), 0)
    live = (tok % GROUP < jnp.where(tok < GROUP, v0, v1)).astype(F32)

    def project(i, _):
        for hh in range(2):
            hd = 2 * i + hh
            lanes = pl.ds(pl.multiple_of(hd * T, T), T)
            qrows = pl.ds(pl.multiple_of(hd * T, T), T)
            q[qrows, :LAT] = nn(nope[:, lanes], wuk[hd]).astype(BF)
            pairs = rope[:, pl.ds(pl.multiple_of(i * 2 * ROPE, 2 * ROPE), 2 * ROPE)]
            q[qrows, LAT:] = pairs[:, hh * ROPE:(hh + 1) * ROPE]
            live_grad = (gh[:, lanes].astype(F32) * live).astype(BF)
            gl[:, lanes] = live_grad
            glt[:, lanes] = nt(wuv[hd], live_grad).astype(BF)
        return 0

    lax.fori_loop(0, H // 2, project, 0, unroll=True)
    pl.semaphore_wait(bar, len(partners))

    near_view = rows(y, zh, c, hx)
    far_view = rows(y, ozh, c, hx)
    xn = (x + 1 + 2 * c) % 4

    def near_copy(i, j):
        return rc(near_view, near_view, sn.at[i * 3 + j - 1], rn.at[i * 3 + 3 - j],
                  dev(xn if i else x, yk(j), zh, zl, c))

    def far_copy(i, j):
        return rc(far_view, far_view, sf.at[i * 4 + j], rf.at[i * 4 + (4 - j) % 4],
                  dev(xn if i else x, yk(j), zh, zl, c))

    near_all = [(1, 2), (0, 2), (1, 1), (1, 3), (0, 1), (0, 3)]
    far_all = near_all + [(1, 0)]

    def z_copy(to_zl, i):
        return rc(near_view, near_view, sz.at[i], rz.at[0], dev(x, y, ozh, to_zl, c))

    @pl.when(zl == 3)
    def _():
        z_copy(1, 1).start()
        z_copy(0, 0).start()

    @pl.when(zl == 0)
    def _():
        z_copy(2, 1).start()
        z_copy(3, 0).start()

    for i, j in near_all:
        near_copy(i, j).start()

    def c_send(zr_, r):
        view = rows(yk(r), zh if zr_ == 0 else ozh, c)
        return rc(view, view, scc.at[zr_ * 4 + r], rcc.at[zr_ * 4 + r], sib)

    def c_wait(zr_, r):
        arrived(rows(yk(r), zh if zr_ == 0 else ozh, oc), rcc.at[zr_ * 4 + r])

    c_send(0, 0).start()
    mx[...] = jnp.full_like(mx, -1e30)

    def scores(base, n, masked):
        def one(i, _):
            cols = pl.ds(pl.multiple_of(i * PAIR, PAIR), PAIR)
            sv = nt(kall[pl.ds(base, n), :], q[cols, :])
            if masked:
                j = lax.broadcasted_iota(jnp.int32, (n, PAIR), 0)
                t = lax.broadcasted_iota(jnp.int32, (n, PAIR), 1) % T
                lim = jnp.where(j < GROUP, v0, GROUP + v1)
                low = jnp.where(t < GROUP, 0, GROUP)
                sv = jnp.where((j <= t) & (j >= low) & (j < lim), sv, -1e30)
            s[pl.ds(base, n), cols] = sv
            mx[:, cols] = jnp.maximum(mx[:, cols], jnp.max(sv.reshape(n // 8, 8, PAIR), axis=0))
            gp[pl.ds(base, n), cols] = nn(kall[pl.ds(base, n), :LAT], glt[:, cols])
            return 0

        lax.fori_loop(0, R // PAIR, one, 0, unroll=True)

    def prompt_scores(base):
        base = pl.multiple_of(base, 128)
        kt[:, pl.ds(base, 384)] = kall[pl.ds(base, 384), :].T
        scores(base, 384, False)

    kall[KP:KA, :] = kt[:, KP:KA].T
    scores(KP, T, True)

    arrived(far_view, rz.at[0])
    for i, j in far_all:
        far_copy(i, j).start()
    for r in (1, 3, 2):
        for i in range(2):
            arrived(rows(yk(r), zh, c, 1 - hx if i else hx), rn.at[i * 3 + r - 1])
        c_send(0, r).start()
    prompt_scores(zh * 768 + c * 384)
    for r in range(4):
        c_wait(0, r)
    prompt_scores(zh * 768 + oc * 384)
    for r in (0, 1, 3, 2):
        for i in range(2):
            if i + r > 0:
                arrived(rows(yk(r), ozh, c, 1 - hx if i else hx), rf.at[i * 4 + r])
        c_send(1, r).start()
    prompt_scores(ozh * 768 + c * 384)
    for r in range(4):
        c_wait(1, r)
    prompt_scores(ozh * 768 + oc * 384)

    def wv_copy(i):
        return rc(wvs.at[i], wvc.at[i], swv.at[i], rwv.at[i], sib)

    def wk_copy(i):
        return rc(wks.at[i], wkc.at[i], swk.at[i], rwk.at[i], sib)

    def y_hop(i, k, buf, rbuf, ssem, rsem):
        n = 4 + 3 * i + k - 1
        return rc(buf.at[i, yk(k)], rbuf.at[i, k - 1], ssem.at[n], rsem.at[n], dev(x, yk(k), zh, zl, c))

    def z_hop(i, buf, rbuf, ssem, rsem):
        return rc(buf.at[i], rbuf.at[i], ssem.at[16 + i], rsem.at[16 + i], dev(x, y, ozh, zl, c))

    def wv_pair(i):
        wv_copy(i).wait_recv()
        t = wvacc[i] + wvc[i].astype(F32)
        wvacc[i] = t
        wvy[i] = t.astype(BF)
        for k in (2, 1, 3):
            y_hop(i, k, wvy, wvr, swv, rwv).start()

    def wk_pair(i):
        wk_copy(i).wait_recv()
        t = wkacc[i] + wkc[i].astype(F32)
        wkacc[i] = t
        wky[i] = t.astype(BF)
        for k in (2, 1, 3):
            y_hop(i, k, wky, wkr, swk, rwk).start()

    STEP = 128

    def softmax(i, _):
        cols = pl.ds(pl.multiple_of(i * PAIR, PAIR), PAIR)
        top = jnp.max(mx[:, cols], axis=0, keepdims=True)

        top = top * EXP2
        acc = jnp.zeros((8, PAIR), F32)
        for j in range(KA // STEP):
            rws = pl.ds(j * STEP, STEP)
            e = jnp.exp2(s[rws, cols] * EXP2 - top)
            s[rws, cols] = e
            low = e.astype(BF)
            p[rws, cols] = low
            acc = acc + jnp.sum(e.reshape(STEP // 8, 8, PAIR), axis=0)
        inv = 1.0 / jnp.sum(acc, axis=0, keepdims=True)
        lot = (nn(kt[:LAT, :], p[:, cols]) * inv).astype(BF)
        grad_latent = glt[:, cols].astype(F32)
        delta = jnp.sum(grad_latent * lot.astype(F32), axis=0, keepdims=True)
        glp[:, cols] = (grad_latent * inv).astype(BF)
        inv = inv * SCALE
        for j in range(KA // STEP):
            rws = pl.ds(j * STEP, STEP)
            ds[rws, cols] = (s[rws, cols] * inv * (gp[rws, cols] - delta)).astype(BF)
        for hh in range(2):
            lanes = pl.ds(pl.multiple_of((2 * i + hh) * T, T), T)
            wvt[...] = nn(lot[:, hh * T:(hh + 1) * T], gl[:, lanes]).reshape(8, 2, 32, VD)
            wvs[i, :, hh] = wvt[:, oc].reshape(4, 2, 32, VD).astype(BF)
            wvacc[i, :, hh] = wvt[:, c].reshape(4, 2, 32, VD)
        wv_copy(i).start()

        @pl.when(i > 0)
        def _():
            wv_pair(i - 1)

        return 0

    lax.fori_loop(0, R // PAIR, softmax, 0)

    def key_grad(base, n):
        rws = pl.ds(base, n)
        kq = nn(ds[rws, :], q[...])
        return kq[:, :LAT] + nt(p[rws, :], glp[...]), kq[:, LAT:]

    def owner_head(o):
        return (o // 2) * 4 + 1 + o % 2

    lat, rot = key_grad(KP, T)
    as_[:, :, :LAT] = lat.reshape(8, 16, LAT).astype(BF)
    as_[:, :, LAT:] = rot.reshape(8, 16, ROPE).astype(BF)
    wv_pair(3)
    for o in range(8):
        cp = rc(as_.at[o], ar.at[h], sa1.at[o], ra1.at[h], {"head": owner_head(o), "ans": a})

        @pl.when(h != owner_head(o))
        def _():
            cp.start()

    def gc_copy(i):
        return rc(gs.at[i], gcr.at[i], sgc.at[i], rgc.at[i], sib)

    def xy_copy(yy, xx):
        n = yy * 4 + xx
        m = y * 4 + x
        return rc(xs.at[n], xr.at[m], sxy.at[n], rxy.at[m], dev(xx, yy, zh, zl, c))

    def to_owner(i, zz):
        gc_copy(i).wait_recv()
        for yy in range(4):
            for half in range(2):
                sub = pl.ds(yy * SH + half * 48, 48)
                part = g[sub, :] + gcr[i, sub, :].astype(F32)
                xx = 2 * zz + half
                xs[yy * 4 + xx] = part.astype(BF)
                mine = (yy == y) & (xx == x)

                @pl.when(mine)
                def _():
                    zacc[...] = part

                @pl.when(jnp.logical_not(mine))
                def _():
                    xy_copy(yy, xx).start()

    for i in range(2):
        zz = hx if i == 0 else 1 - hx
        lat, rot = key_grad(pl.multiple_of(zz * 768 + oc * 384, 128), 384)
        gs[i, :, :LAT] = lat.astype(BF)
        gs[i, :, LAT:] = rot.astype(BF)
        gc_copy(i).start()
        lat, rot = key_grad(pl.multiple_of(zz * 768 + c * 384, 128), 384)
        g[:, :LAT] = lat
        g[:, LAT:] = rot
        to_owner(i, zz)

    def wv_mid(i):
        for k in (1, 2, 3):
            y_hop(i, k, wvy, wvr, swv, rwv).wait_recv()
        t = wvacc[i, y]
        for k in (1, 2, 3):
            t = t + wvr[i, k - 1].astype(F32)
        wvz[i] = t
        wvzs[i] = wvz[i, :, ozh].astype(BF)
        z_hop(i, wvzs, wvzr, swv, rwv).start()

    def queries(i, _):
        cols = pl.ds(pl.multiple_of(i * PAIR, PAIR), PAIR)
        gqt = nn(kt[...], ds[:, cols])
        glq = gqt[:LAT].astype(BF)
        rot = gqt[LAT:].T
        for hh in range(2):
            hd = 2 * i + hh
            lanes = pl.ds(pl.multiple_of(hd * T, T), T)
            part = glq[:, hh * T:(hh + 1) * T]
            v_nope[:, lanes] = nn(wuk[hd], part).T.astype(BF)
            nope_t = nope[:, lanes].astype(F32).T.astype(BF)
            wkt[...] = nt(nope_t, part).reshape(8, 2, 8, LAT)
            wks[i, :, hh] = wkt[:, oc].reshape(4, 16, LAT).astype(BF)
            wkacc[i, :, hh] = wkt[:, c].reshape(4, 16, LAT)
        v_rope[:, pl.ds(pl.multiple_of(i * T, T), T)] = jnp.concatenate(
            [rot[:T], rot[T:]], axis=1).astype(BF)
        wk_copy(i).start()

        wv_mid(i)
        return 0

    lax.fori_loop(0, 4, queries, 0)
    out_nope = pltpu.make_async_copy(v_nope, o_nope, sout.at[0])
    out_rope = pltpu.make_async_copy(v_rope, o_rope, sout.at[1])
    out_nope.start()
    out_rope.start()

    me_xy = y * 4 + x
    for i in range(1, 16):
        src = (me_xy + i) % 16
        arrived(xr.at[src], rxy.at[src])
    xr[me_xy] = jnp.zeros((48, W), BF)
    acc = zacc[...]
    for i in range(16):
        acc = acc + xr[i].astype(F32)
    zs[...] = acc.reshape(3, 16, W).astype(BF)
    goal = x // 2
    me_z = zh * 4 + zl

    def zz_copy(i):
        return rc(zs.at[i], zr.at[me_z], szz.at[i], rzz.at[me_z], dev(x, y, goal, i, c))

    for i in range(3):
        @pl.when(me_z != goal * 4 + i)
        def _():
            zz_copy(i).start()

    for i in range(4):
        wk_pair(i)

    is_owner = (zl == 1) | (zl == 2)
    mine = x * 2 + zl - 1

    def answer_out(i):
        return rc(fa, aa.at[mine], sa2.at[i - 1], ra2.at[mine], {"head": (h + i) % 16, "ans": a})

    @pl.when(is_owner)
    def _():
        ar[h] = as_[mine]
        for i in range(1, 16):
            src = (h + i) % 16
            arrived(ar.at[src], ra1.at[src])
        acc = jnp.zeros((16, W), F32)
        for i in range(16):
            acc = acc + ar[i].astype(F32)
        fa[...] = acc.astype(BF)
        for i in range(1, 16):
            answer_out(i).start()
        aa[mine] = fa[...]

    is_src = (zh == goal) & (zl < 3)
    piece = (x % 2) * 3 + zl

    def ag_copy(i):
        return rc(fz, ag.at[piece], sag.at[i - 1], rag.at[piece], {"head": (h + i) % 16, "ans": a})

    @pl.when(is_src)
    def _():
        zr[me_z] = zs[zl]
        for i in range(1, 8):
            src = (me_z + i) % 8
            arrived(zr.at[src], rzz.at[src])
        tot = jnp.zeros((16, W), F32)
        for i in range(8):
            tot = tot + zr[i].astype(F32)
        fz[...] = tot.astype(BF)
        for i in range(1, 16):
            ag_copy(i).start()
        ag[piece] = fz[...]

    def wk_mid(i, _):
        for k in (1, 2, 3):
            y_hop(i, k, wky, wkr, swk, rwk).wait_recv()
        t = wkacc[i, y]
        for k in (1, 2, 3):
            t = t + wkr[i, k - 1].astype(F32)
        wkz[i] = t.reshape(2, 2, 8, LAT)
        wkzs[i] = wkz[i, :, ozh].reshape(16, LAT).astype(BF)
        z_hop(i, wkzs, wkzr, swk, rwk).start()
        return 0

    lax.fori_loop(0, 4, wk_mid, 0)

    for o in range(8):
        @pl.when(h != owner_head(o))
        def _():
            arrived(aa.at[o], ra2.at[o])

    v_ans[...] = aa[...].astype(F32).reshape(T, W).T
    out_ans = pltpu.make_async_copy(v_ans, o_ans, sout.at[2])
    out_ans.start()

    def weights_out(i, _):
        z_hop(i, wvzs, wvzr, swv, rwv).wait_recv()
        v_wv[pl.ds(2 * i, 2)] = wvz[i, :, zh] + wvzr[i].astype(F32)
        z_hop(i, wkzs, wkzr, swk, rwk).wait_recv()
        v_wk[pl.ds(2 * i, 2)] = wkz[i, :, zh] + wkzr[i].astype(F32).reshape(2, 8, LAT)
        return 0

    lax.fori_loop(0, 4, weights_out, 0)
    out_wk = pltpu.make_async_copy(v_wk, o_wk, sout.at[3])
    out_wv = pltpu.make_async_copy(v_wv, o_wv, sout.at[4])
    out_wk.start()
    out_wv.start()

    for zr_ in range(2):
        for r in range(4):
            c_send(zr_, r).wait_send()

    for i, j in near_all:
        near_copy(i, j).wait_send()
    for i, j in far_all:
        far_copy(i, j).wait_send()

    @pl.when((zl == 3) | (zl == 0))
    def _():
        sent(near_view, sz.at[0])
        sent(near_view, sz.at[1])

    for o in range(8):
        @pl.when(h != owner_head(o))
        def _():
            sent(as_.at[o], sa1.at[o])

    @pl.when(is_owner)
    def _():
        for i in range(1, 16):
            sent(fa, sa2.at[i - 1])

    for i in range(3):
        @pl.when(me_z != goal * 4 + i)
        def _():
            sent(zs.at[i], szz.at[i])

    for i in range(1, 16):
        dst = (me_xy + i) % 16
        sent(xs.at[dst], sxy.at[dst])

    for i in range(2):
        gc_copy(i).wait_send()

    def drain(i, _):
        wv_copy(i).wait_send()
        wk_copy(i).wait_send()
        for k in (1, 2, 3):
            y_hop(i, k, wvy, wvr, swv, rwv).wait_send()
            y_hop(i, k, wky, wkr, swk, rwk).wait_send()
        z_hop(i, wvzs, wvzr, swv, rwv).wait_send()
        z_hop(i, wkzs, wkzr, swk, rwk).wait_send()
        return 0

    lax.fori_loop(0, 4, drain, 0)

    for i in range(6):
        @pl.when(h != (2 * zh + i // 3) * 4 + i % 3)
        def _():
            arrived(ag.at[i], rag.at[i])

    v_prm[...] = ag[...].astype(F32).reshape(SH, W)
    out_prm = pltpu.make_async_copy(v_prm, o_prm, sout.at[5])
    out_prm.start()

    @pl.when(is_src)
    def _():
        for i in range(1, 16):
            sent(fz, sag.at[i - 1])

    for cp in (out_nope, out_rope, out_ans, out_wk, out_wv, out_prm):
        cp.wait()


def hand_over(*refs):
    for i in range(6):
        refs[6 + i][...] = refs[i][...]


def per_device(nope, rope, ans, *rest):
    V = pltpu.VMEM
    D = pltpu.SemaphoreType.DMA
    outs = (
        jax.ShapeDtypeStruct((T, H * HD), BF),
        jax.ShapeDtypeStruct((T, H * ROPE), BF),
        jax.ShapeDtypeStruct((W, T), F32),
        jax.ShapeDtypeStruct((SH, W), F32),
        jax.ShapeDtypeStruct((H, 8, LAT), F32),
        jax.ShapeDtypeStruct((H, 32, VD), F32),
    )
    scratch = [
        V((T, H * HD), BF), V((T, H * ROPE), BF), V((H, HD, LAT), BF), V((H, LAT, VD), BF), V((T, H * VD), BF),
    ] + [V(o.shape, o.dtype) for o in outs] + [
        V((KA, W), BF), V((W, KA), BF), V((R, W), BF), V((LAT, R), BF), V((LAT, R), BF), V((T, H * VD), BF),
        V((KA, R), F32), V((KA, R), F32), V((KA, R), BF), V((KA, R), BF), V((8, R), F32), V((384, W), F32),
        V((2, 384, W), BF), V((2, 384, W), BF), V((16, 48, W), BF), V((16, 48, W), BF), V((48, W), F32),
        V((3, 16, W), BF), V((8, 16, W), BF), V((16, W), BF), V((6, 16, W), BF),
        V((8, 16, W), BF), V((16, 16, W), BF), V((16, W), BF), V((8, 16, W), BF),
        V((8, 2, 32, VD), F32), V((4, 4, 2, 2, 32, VD), BF), V((4, 4, 2, 2, 32, VD), BF),
        V((4, 4, 2, 2, 32, VD), F32), V((4, 4, 2, 2, 32, VD), BF), V((4, 3, 2, 2, 32, VD), BF),
        V((4, 2, 2, 32, VD), F32), V((4, 2, 32, VD), BF), V((4, 2, 32, VD), BF),
        V((8, 2, 8, LAT), F32), V((4, 4, 2, 16, LAT), BF), V((4, 4, 2, 16, LAT), BF),
        V((4, 4, 2, 16, LAT), F32), V((4, 4, 2, 16, LAT), BF), V((4, 3, 2, 16, LAT), BF),
        V((4, 2, 2, 8, LAT), F32), V((4, 16, LAT), BF), V((4, 16, LAT), BF),
        D((7,)), D((6,)),
        D((2,)), D((1,)), D((6,)), D((6,)), D((8,)), D((8,)), D((8,)), D((8,)),
        D((2,)), D((2,)), D((16,)), D((16,)), D((3,)), D((8,)), D((15,)), D((6,)),
        D((8,)), D((16,)), D((15,)), D((8,)),
        D((20,)), D((20,)), D((20,)), D((20,)),
    ]
    hbm = pl.BlockSpec(memory_space=pl.ANY)
    got = pl.pallas_call(
        kernel,
        out_shape=outs,
        in_specs=[hbm] * 7 + [pl.BlockSpec(memory_space=pltpu.SMEM)],
        out_specs=(hbm,) * 6,
        scratch_shapes=scratch,
        compiler_params=pltpu.CompilerParams(
            collective_id=0, has_side_effects=True, vmem_limit_bytes=62 * 1024 * 1024
        ),
    )(nope, rope, ans.T, *rest)
    res = pl.pallas_call(
        hand_over,
        out_shape=outs,
        in_specs=[pl.BlockSpec(memory_space=pltpu.VMEM)] * 6,
        out_specs=(pl.BlockSpec(memory_space=pltpu.VMEM),) * 6,
    )(*got)
    return res[0], res[1], res[2].T, res[3], res[4], res[5]


def solution(mesh):
    return jax.shard_map(
        per_device,
        mesh=mesh,
        in_specs=(
            P("ans", "head"),
            P("ans", "head"),
            P("ans", None),
            P("ans", None),
            P("head", None, None),
            P("head", None, None),
            P("ans", "head"),
            P("ans"),
        ),
        out_specs=(
            P("ans", "head"),
            P("ans", "head"),
            P("ans", None),
            P("ans", None),
            P("head", "ans", None),
            P("head", "ans", None),
        ),
        check_vma=False,
    )
```

```python
import jax
import jax.numpy as jnp
from jax import lax
from jax.experimental import pallas as pl
from jax.experimental.pallas import tpu as pltpu
from jax.sharding import PartitionSpec as P

LAT = 512
ROPE = 64
HD = 128
VD = 128
GROUP = 64
W = LAT + ROPE
MESH = pl.DeviceIdType.MESH
F32 = jnp.float32
BF = jnp.bfloat16
SCALE = (HD + ROPE) ** (-0.5)
EXP2 = SCALE * 1.4426950408889634

T = 128
H = 8
R = T * H
SH = 96
KP = 1536
KA = KP + T
PAIR = 2 * T


def nn(a, b):
    return jnp.dot(a, b, preferred_element_type=F32)


def nt(a, b):
    return lax.dot_general(a, b, (((1,), (1,)), ((), ())), preferred_element_type=F32)


def kernel(
    nope_in, rope_in, ans_in, prm_in, wuk_in, wuv_in, gh_in, valid,
    o_nope, o_rope, o_ans, o_prm, o_wk, o_wv,
    nope, rope, wuk, wuv, gh, v_nope, v_rope, v_ans, v_prm, v_wk, v_wv,
    kall, kt, q, glt, glp, gl, s, gp, p, ds, mx, g,
    gs, gcr, xs, xr, zacc, zs, zr, fz, ag,
    as_, ar, fa, aa,
    wvt, wvs, wvc, wvacc, wvy, wvr, wvz, wvzs, wvzr,
    wkt, wks, wkc, wkacc, wky, wkr, wkz, wkzs, wkzr,
    sin, sout,
    sz, rz, sn, rn, sf, rf, scc, rcc,
    sgc, rgc, sxy, rxy, szz, rzz, sag, rag,
    sa1, ra1, sa2, ra2,
    swv, rwv, swk, rwk,
):
    h = lax.axis_index("head")
    a = lax.axis_index("ans")
    x, zl = h // 4, h % 4
    y, zh, c = a // 4, (a // 2) % 2, a % 2
    oc, ozh = 1 - c, 1 - zh
    hx = x % 2

    def dev(x_, y_, zh_, zl_, c_):
        return {"head": x_ * 4 + zl_, "ans": y_ * 4 + zh_ * 2 + c_}

    sib = dev(x, y, zh, zl, oc)

    def rc(src, dst, ss, rs, d):
        return pltpu.make_async_remote_copy(
            src_ref=src, dst_ref=dst, send_sem=ss, recv_sem=rs, device_id=d, device_id_type=MESH
        )

    def arrived(dst, rs):
        rc(dst, dst, rs, rs, sib).wait_recv()

    def sent(src, ss):
        rc(src, src, ss, ss, sib).wait_send()

    def yk(k):
        return (y + k) % 4

    partners = [dev((x + i) % 4, (y + j) % 4, zh, zl, c) for i in range(4) for j in range(4) if i + j > 0]
    partners += [dev((x + i) % 4, y, zh, (zl + j) % 4, c) for i in range(4) for j in range(1, 4)]
    partners += [dev(x, y, ozh, i, c) for i in range(4)] + [sib]
    bar = pltpu.get_barrier_semaphore()
    for d in partners:
        pl.semaphore_signal(bar, inc=1, device_id=d, device_id_type=MESH)

    def rows(y_, zh_, c_, half=None):
        base = zh_ * 768 + c_ * 384 + y_ * SH
        if half is None:
            return kall.at[pl.ds(pl.multiple_of(base, 16), SH)]
        return kall.at[pl.ds(pl.multiple_of(base + half * 48, 16), 48)]

    loads = [
        pltpu.make_async_copy(src, dst, sin.at[i])
        for i, (src, dst) in enumerate(
            [(prm_in, rows(y, zh, c)), (nope_in, nope), (rope_in, rope), (wuk_in, wuk), (wuv_in, wuv),
             (gh_in, gh), (ans_in, kt.at[:, pl.ds(KP, T)])]
        )
    ]
    for cp in loads:
        cp.start()
    for cp in loads:
        cp.wait()

    v0, v1 = valid[0], valid[1]
    tok = lax.broadcasted_iota(jnp.int32, (T, T), 0)
    live = (tok % GROUP < jnp.where(tok < GROUP, v0, v1)).astype(F32)

    def project(i, _):
        for hh in range(2):
            hd = 2 * i + hh
            lanes = pl.ds(pl.multiple_of(hd * T, T), T)
            qrows = pl.ds(pl.multiple_of(hd * T, T), T)
            q[qrows, :LAT] = nn(nope[:, lanes], wuk[hd]).astype(BF)
            pairs = rope[:, pl.ds(pl.multiple_of(i * 2 * ROPE, 2 * ROPE), 2 * ROPE)]
            q[qrows, LAT:] = pairs[:, hh * ROPE:(hh + 1) * ROPE]
            live_grad = (gh[:, lanes].astype(F32) * live).astype(BF)
            gl[:, lanes] = live_grad
            glt[:, lanes] = nt(wuv[hd], live_grad).astype(BF)
        return 0

    lax.fori_loop(0, H // 2, project, 0, unroll=True)
    pl.semaphore_wait(bar, len(partners))

    near_view = rows(y, zh, c, hx)
    far_view = rows(y, ozh, c, hx)
    xn = (x + 1 + 2 * c) % 4

    def near_copy(i, j):
        return rc(near_view, near_view, sn.at[i * 3 + j - 1], rn.at[i * 3 + 3 - j],
                  dev(xn if i else x, yk(j), zh, zl, c))

    def far_copy(i, j):
        return rc(far_view, far_view, sf.at[i * 4 + j], rf.at[i * 4 + (4 - j) % 4],
                  dev(xn if i else x, yk(j), zh, zl, c))

    near_all = [(1, 2), (0, 2), (1, 1), (1, 3), (0, 1), (0, 3)]
    far_all = near_all + [(1, 0)]

    def z_copy(to_zl, i):
        return rc(near_view, near_view, sz.at[i], rz.at[0], dev(x, y, ozh, to_zl, c))

    @pl.when(zl == 3)
    def _():
        z_copy(1, 1).start()
        z_copy(0, 0).start()

    @pl.when(zl == 0)
    def _():
        z_copy(2, 1).start()
        z_copy(3, 0).start()

    for i, j in near_all:
        near_copy(i, j).start()

    def c_send(zr_, r):
        view = rows(yk(r), zh if zr_ == 0 else ozh, c)
        return rc(view, view, scc.at[zr_ * 4 + r], rcc.at[zr_ * 4 + r], sib)

    def c_wait(zr_, r):
        arrived(rows(yk(r), zh if zr_ == 0 else ozh, oc), rcc.at[zr_ * 4 + r])

    c_send(0, 0).start()
    mx[...] = jnp.full_like(mx, -1e30)

    def scores(base, n, masked):
        def one(i, _):
            cols = pl.ds(pl.multiple_of(i * PAIR, PAIR), PAIR)
            sv = nt(kall[pl.ds(base, n), :], q[cols, :])
            if masked:
                j = lax.broadcasted_iota(jnp.int32, (n, PAIR), 0)
                t = lax.broadcasted_iota(jnp.int32, (n, PAIR), 1) % T
                lim = jnp.where(j < GROUP, v0, GROUP + v1)
                low = jnp.where(t < GROUP, 0, GROUP)
                sv = jnp.where((j <= t) & (j >= low) & (j < lim), sv, -1e30)
            s[pl.ds(base, n), cols] = sv
            mx[:, cols] = jnp.maximum(mx[:, cols], jnp.max(sv.reshape(n // 8, 8, PAIR), axis=0))
            gp[pl.ds(base, n), cols] = nn(kall[pl.ds(base, n), :LAT], glt[:, cols])
            return 0

        lax.fori_loop(0, R // PAIR, one, 0, unroll=True)

    def prompt_scores(base):
        base = pl.multiple_of(base, 128)
        kt[:, pl.ds(base, 384)] = kall[pl.ds(base, 384), :].T
        scores(base, 384, False)

    kall[KP:KA, :] = kt[:, KP:KA].T
    scores(KP, T, True)

    arrived(far_view, rz.at[0])
    for i, j in far_all:
        far_copy(i, j).start()
    for r in (1, 3, 2):
        for i in range(2):
            arrived(rows(yk(r), zh, c, 1 - hx if i else hx), rn.at[i * 3 + r - 1])
        c_send(0, r).start()
    prompt_scores(zh * 768 + c * 384)
    for r in range(4):
        c_wait(0, r)
    prompt_scores(zh * 768 + oc * 384)
    for r in (0, 1, 3, 2):
        for i in range(2):
            if i + r > 0:
                arrived(rows(yk(r), ozh, c, 1 - hx if i else hx), rf.at[i * 4 + r])
        c_send(1, r).start()
    prompt_scores(ozh * 768 + c * 384)
    for r in range(4):
        c_wait(1, r)
    prompt_scores(ozh * 768 + oc * 384)

    def wv_copy(i):
        return rc(wvs.at[i], wvc.at[i], swv.at[i], rwv.at[i], sib)

    def wk_copy(i):
        return rc(wks.at[i], wkc.at[i], swk.at[i], rwk.at[i], sib)

    def y_hop(i, k, buf, rbuf, ssem, rsem):
        n = 4 + 3 * i + k - 1
        return rc(buf.at[i, yk(k)], rbuf.at[i, k - 1], ssem.at[n], rsem.at[n], dev(x, yk(k), zh, zl, c))

    def z_hop(i, buf, rbuf, ssem, rsem):
        return rc(buf.at[i], rbuf.at[i], ssem.at[16 + i], rsem.at[16 + i], dev(x, y, ozh, zl, c))

    def wv_pair(i):
        wv_copy(i).wait_recv()
        t = wvacc[i] + wvc[i].astype(F32)
        wvacc[i] = t
        wvy[i] = t.astype(BF)
        for k in (2, 1, 3):
            y_hop(i, k, wvy, wvr, swv, rwv).start()

    def wk_pair(i):
        wk_copy(i).wait_recv()
        t = wkacc[i] + wkc[i].astype(F32)
        wkacc[i] = t
        wky[i] = t.astype(BF)
        for k in (2, 1, 3):
            y_hop(i, k, wky, wkr, swk, rwk).start()

    STEP = 128

    def softmax(i, _):
        cols = pl.ds(pl.multiple_of(i * PAIR, PAIR), PAIR)
        top = jnp.max(mx[:, cols], axis=0, keepdims=True)

        top = top * EXP2
        acc = jnp.zeros((8, PAIR), F32)
        for j in range(KA // STEP):
            rws = pl.ds(j * STEP, STEP)
            e = jnp.exp2(s[rws, cols] * EXP2 - top)
            s[rws, cols] = e
            low = e.astype(BF)
            p[rws, cols] = low
            acc = acc + jnp.sum(e.reshape(STEP // 8, 8, PAIR), axis=0)
        inv = 1.0 / jnp.sum(acc, axis=0, keepdims=True)
        lot = (nn(kt[:LAT, :], p[:, cols]) * inv).astype(BF)
        grad_latent = glt[:, cols].astype(F32)
        delta = jnp.sum(grad_latent * lot.astype(F32), axis=0, keepdims=True)
        glp[:, cols] = (grad_latent * inv).astype(BF)
        inv = inv * SCALE
        for j in range(KA // STEP):
            rws = pl.ds(j * STEP, STEP)
            ds[rws, cols] = (s[rws, cols] * inv * (gp[rws, cols] - delta)).astype(BF)
        for hh in range(2):
            lanes = pl.ds(pl.multiple_of((2 * i + hh) * T, T), T)
            wvt[...] = nn(lot[:, hh * T:(hh + 1) * T], gl[:, lanes]).reshape(8, 2, 32, VD)
            wvs[i, :, hh] = wvt[:, oc].reshape(4, 2, 32, VD).astype(BF)
            wvacc[i, :, hh] = wvt[:, c].reshape(4, 2, 32, VD)
        wv_copy(i).start()

        @pl.when(i > 0)
        def _():
            wv_pair(i - 1)

        return 0

    lax.fori_loop(0, R // PAIR, softmax, 0)

    def key_grad(base, n):
        rws = pl.ds(base, n)
        kq = nn(ds[rws, :], q[...])
        return kq[:, :LAT] + nt(p[rws, :], glp[...]), kq[:, LAT:]

    def owner_head(o):
        return (o // 2) * 4 + 1 + o % 2

    lat, rot = key_grad(KP, T)
    as_[:, :, :LAT] = lat.reshape(8, 16, LAT).astype(BF)
    as_[:, :, LAT:] = rot.reshape(8, 16, ROPE).astype(BF)
    wv_pair(3)
    for o in range(8):
        cp = rc(as_.at[o], ar.at[h], sa1.at[o], ra1.at[h], {"head": owner_head(o), "ans": a})

        @pl.when(h != owner_head(o))
        def _():
            cp.start()

    def gc_copy(i):
        return rc(gs.at[i], gcr.at[i], sgc.at[i], rgc.at[i], sib)

    def xy_copy(zz, yy, xx):
        n = zz * 16 + yy * 4 + xx
        m = zz * 16 + y * 4 + x
        return rc(xs.at[n], xr.at[m], sxy.at[n], rxy.at[m], dev(xx, yy, zh, zl, c))

    def to_owner(i, zz, ys):
        for yy in ys:
            sub = pl.ds(yy * SH, SH)
            t = g[sub, :] + gcr[i, sub, :].astype(F32)
            for xx in range(4):
                lat = t[:, xx * 128:(xx + 1) * 128]
                if xx < 3:
                    rot = t[32 * xx:32 * xx + 32, LAT:]
                    rot = jnp.concatenate([rot[:16], rot[16:]], axis=1)
                else:
                    rot = jnp.zeros((16, 128), F32)
                n = zz * 16 + yy * 4 + xx
                xs[n, :SH] = lat.astype(BF)
                xs[n, SH:] = rot.astype(BF)
                mine = (yy == y) & (xx == x)

                @pl.when(mine)
                def _():
                    zacc[zz, :SH] = lat
                    zacc[zz, SH:] = rot

                @pl.when(jnp.logical_not(mine))
                def _():
                    xy_copy(zz, yy, xx).start()

    for i in range(2):
        zz = hx if i == 0 else 1 - hx
        lat, rot = key_grad(pl.multiple_of(zz * 768 + oc * 384, 128), 384)
        gs[i, :, :LAT] = lat.astype(BF)
        gs[i, :, LAT:] = rot.astype(BF)
        gc_copy(i).start()
        lat, rot = key_grad(pl.multiple_of(zz * 768 + c * 384, 128), 384)
        g[:, :LAT] = lat
        g[:, LAT:] = rot
        gc_copy(i).wait_recv()
        to_owner(i, zz, range(4))

    def wv_mid(i):
        for k in (1, 2, 3):
            y_hop(i, k, wvy, wvr, swv, rwv).wait_recv()
        t = wvacc[i, y]
        for k in (1, 2, 3):
            t = t + wvr[i, k - 1].astype(F32)
        wvz[i] = t
        wvzs[i] = wvz[i, :, ozh].astype(BF)
        z_hop(i, wvzs, wvzr, swv, rwv).start()

    def queries(i, _):
        cols = pl.ds(pl.multiple_of(i * PAIR, PAIR), PAIR)
        gqt = nn(kt[...], ds[:, cols])
        glq = gqt[:LAT].astype(BF)
        rot = gqt[LAT:].T
        for hh in range(2):
            hd = 2 * i + hh
            lanes = pl.ds(pl.multiple_of(hd * T, T), T)
            part = glq[:, hh * T:(hh + 1) * T]
            v_nope[:, lanes] = nn(wuk[hd], part).T.astype(BF)
            nope_t = nope[:, lanes].astype(F32).T.astype(BF)
            wkt[...] = nt(nope_t, part).reshape(8, 2, 8, LAT)
            wks[i, :, hh] = wkt[:, oc].reshape(4, 16, LAT).astype(BF)
            wkacc[i, :, hh] = wkt[:, c].reshape(4, 16, LAT)
        v_rope[:, pl.ds(pl.multiple_of(i * T, T), T)] = jnp.concatenate(
            [rot[:T], rot[T:]], axis=1).astype(BF)
        wk_copy(i).start()

        wv_mid(i)
        return 0

    lax.fori_loop(0, 4, queries, 0)
    out_nope = pltpu.make_async_copy(v_nope, o_nope, sout.at[0])
    out_rope = pltpu.make_async_copy(v_rope, o_rope, sout.at[1])
    out_nope.start()
    out_rope.start()

    for i in range(4):
        wk_pair(i)

    me_xy = y * 4 + x
    me_z = zh * 4 + zl

    def zz_copy(n):
        return rc(zs.at[n], zr.at[me_z], szz.at[n], rzz.at[me_z], dev(x, y, n // 4, n % 4, c))

    for zz in (hx, 1 - hx):
        for i in range(1, 16):
            src = zz * 16 + (me_xy + i) % 16
            arrived(xr.at[src], rxy.at[src])
        xr[zz * 16 + me_xy] = jnp.zeros((SH + 16, 128), BF)
        acc = zacc[zz]
        for i in range(16):
            acc = acc + xr[zz * 16 + i].astype(F32)
        acc = acc.astype(BF)
        for i in range(3):
            zs[zz * 4 + i] = acc[32 * i:32 * i + 32]
        zs[zz * 4 + 3, :16] = acc[SH:]
        zs[zz * 4 + 3, 16:] = jnp.zeros((16, 128), BF)
        for i in range(4):
            @pl.when(me_z != zz * 4 + i)
            def _():
                zz_copy(zz * 4 + i).start()

    is_owner = (zl == 1) | (zl == 2)
    mine = x * 2 + zl - 1

    def answer_out(i):
        return rc(fa, aa.at[mine], sa2.at[i - 1], ra2.at[mine], {"head": (h + i) % 16, "ans": a})

    @pl.when(is_owner)
    def _():
        ar[h] = as_[mine]
        for i in range(1, 16):
            src = (h + i) % 16
            arrived(ar.at[src], ra1.at[src])
        acc = jnp.zeros((16, W), F32)
        for i in range(16):
            acc = acc + ar[i].astype(F32)
        fa[...] = acc.astype(BF)
        for i in range(1, 16):
            answer_out(i).start()
        aa[mine] = fa[...]

    def ag_copy(i):
        return rc(fz, ag.at[h], sag.at[i - 1], rag.at[h], {"head": (h + i) % 16, "ans": a})

    zr[me_z] = zs[me_z]
    for i in range(1, 8):
        src = (me_z + i) % 8
        arrived(zr.at[src], rzz.at[src])
    tot = jnp.zeros((32, 128), F32)
    for i in range(8):
        tot = tot + zr[i].astype(F32)
    fz[...] = tot.astype(BF)
    for i in range(1, 16):
        ag_copy(i).start()
    ag[h] = fz[...]

    def wk_mid(i, _):
        for k in (1, 2, 3):
            y_hop(i, k, wky, wkr, swk, rwk).wait_recv()
        t = wkacc[i, y]
        for k in (1, 2, 3):
            t = t + wkr[i, k - 1].astype(F32)
        wkz[i] = t.reshape(2, 2, 8, LAT)
        wkzs[i] = wkz[i, :, ozh].reshape(16, LAT).astype(BF)
        z_hop(i, wkzs, wkzr, swk, rwk).start()
        return 0

    lax.fori_loop(0, 4, wk_mid, 0)

    for o in range(8):
        @pl.when(h != owner_head(o))
        def _():
            arrived(aa.at[o], ra2.at[o])

    v_ans[...] = aa[...].astype(F32).reshape(T, W).T
    out_ans = pltpu.make_async_copy(v_ans, o_ans, sout.at[2])
    out_ans.start()

    def weights_out(i, _):
        z_hop(i, wvzs, wvzr, swv, rwv).wait_recv()
        v_wv[pl.ds(2 * i, 2)] = wvz[i, :, zh] + wvzr[i].astype(F32)
        z_hop(i, wkzs, wkzr, swk, rwk).wait_recv()
        v_wk[pl.ds(2 * i, 2)] = wkz[i, :, zh] + wkzr[i].astype(F32).reshape(2, 8, LAT)
        return 0

    lax.fori_loop(0, 4, weights_out, 0)
    out_wk = pltpu.make_async_copy(v_wk, o_wk, sout.at[3])
    out_wv = pltpu.make_async_copy(v_wv, o_wv, sout.at[4])
    out_wk.start()
    out_wv.start()

    for zr_ in range(2):
        for r in range(4):
            c_send(zr_, r).wait_send()

    for i, j in near_all:
        near_copy(i, j).wait_send()
    for i, j in far_all:
        far_copy(i, j).wait_send()

    @pl.when((zl == 3) | (zl == 0))
    def _():
        sent(near_view, sz.at[0])
        sent(near_view, sz.at[1])

    for o in range(8):
        @pl.when(h != owner_head(o))
        def _():
            sent(as_.at[o], sa1.at[o])

    @pl.when(is_owner)
    def _():
        for i in range(1, 16):
            sent(fa, sa2.at[i - 1])

    for i in range(8):
        @pl.when(me_z != i)
        def _():
            sent(zs.at[i], szz.at[i])

    for zz in range(2):
        for i in range(1, 16):
            dst = zz * 16 + (me_xy + i) % 16
            sent(xs.at[dst], sxy.at[dst])

    for i in range(2):
        gc_copy(i).wait_send()

    def drain(i, _):
        wv_copy(i).wait_send()
        wk_copy(i).wait_send()
        for k in (1, 2, 3):
            y_hop(i, k, wvy, wvr, swv, rwv).wait_send()
            y_hop(i, k, wky, wkr, swk, rwk).wait_send()
        z_hop(i, wvzs, wvzr, swv, rwv).wait_send()
        z_hop(i, wkzs, wkzr, swk, rwk).wait_send()
        return 0

    lax.fori_loop(0, 4, drain, 0)

    for i in range(1, 16):
        src = (h + i) % 16
        arrived(ag.at[src], rag.at[src])

    for xx in range(4):
        for i in range(3):
            v_prm[32 * i:32 * i + 32, 128 * xx:128 * xx + 128] = ag[xx * 4 + i].astype(F32)
        if xx < 3:
            rot = ag[xx * 4 + 3].astype(F32)
            v_prm[32 * xx:32 * xx + 16, LAT:] = rot[:16, :ROPE]
            v_prm[32 * xx + 16:32 * xx + 32, LAT:] = rot[:16, ROPE:]
    out_prm = pltpu.make_async_copy(v_prm, o_prm, sout.at[5])
    out_prm.start()

    for i in range(1, 16):
        sent(fz, sag.at[i - 1])

    for cp in (out_nope, out_rope, out_ans, out_wk, out_wv, out_prm):
        cp.wait()


def hand_over(*refs):
    for i in range(6):
        refs[6 + i][...] = refs[i][...]


def per_device(nope, rope, ans, *rest):
    V = pltpu.VMEM
    D = pltpu.SemaphoreType.DMA
    outs = (
        jax.ShapeDtypeStruct((T, H * HD), BF),
        jax.ShapeDtypeStruct((T, H * ROPE), BF),
        jax.ShapeDtypeStruct((W, T), F32),
        jax.ShapeDtypeStruct((SH, W), F32),
        jax.ShapeDtypeStruct((H, 8, LAT), F32),
        jax.ShapeDtypeStruct((H, 32, VD), F32),
    )
    scratch = [
        V((T, H * HD), BF), V((T, H * ROPE), BF), V((H, HD, LAT), BF), V((H, LAT, VD), BF), V((T, H * VD), BF),
    ] + [V(o.shape, o.dtype) for o in outs] + [
        V((KA, W), BF), V((W, KA), BF), V((R, W), BF), V((LAT, R), BF), V((LAT, R), BF), V((T, H * VD), BF),
        V((KA, R), F32), V((KA, R), F32), V((KA, R), BF), V((KA, R), BF), V((8, R), F32), V((384, W), F32),
        V((2, 384, W), BF), V((2, 384, W), BF), V((32, SH + 16, 128), BF), V((32, SH + 16, 128), BF), V((2, SH + 16, 128), F32),
        V((8, 32, 128), BF), V((8, 32, 128), BF), V((32, 128), BF), V((16, 32, 128), BF),
        V((8, 16, W), BF), V((16, 16, W), BF), V((16, W), BF), V((8, 16, W), BF),
        V((8, 2, 32, VD), F32), V((4, 4, 2, 2, 32, VD), BF), V((4, 4, 2, 2, 32, VD), BF),
        V((4, 4, 2, 2, 32, VD), F32), V((4, 4, 2, 2, 32, VD), BF), V((4, 3, 2, 2, 32, VD), BF),
        V((4, 2, 2, 32, VD), F32), V((4, 2, 32, VD), BF), V((4, 2, 32, VD), BF),
        V((8, 2, 8, LAT), F32), V((4, 4, 2, 16, LAT), BF), V((4, 4, 2, 16, LAT), BF),
        V((4, 4, 2, 16, LAT), F32), V((4, 4, 2, 16, LAT), BF), V((4, 3, 2, 16, LAT), BF),
        V((4, 2, 2, 8, LAT), F32), V((4, 16, LAT), BF), V((4, 16, LAT), BF),
        D((7,)), D((6,)),
        D((2,)), D((1,)), D((6,)), D((6,)), D((8,)), D((8,)), D((8,)), D((8,)),
        D((2,)), D((2,)), D((32,)), D((32,)), D((8,)), D((8,)), D((15,)), D((16,)),
        D((8,)), D((16,)), D((15,)), D((8,)),
        D((20,)), D((20,)), D((20,)), D((20,)),
    ]
    hbm = pl.BlockSpec(memory_space=pl.ANY)
    got = pl.pallas_call(
        kernel,
        out_shape=outs,
        in_specs=[hbm] * 7 + [pl.BlockSpec(memory_space=pltpu.SMEM)],
        out_specs=(hbm,) * 6,
        scratch_shapes=scratch,
        compiler_params=pltpu.CompilerParams(
            collective_id=0, has_side_effects=True, vmem_limit_bytes=62 * 1024 * 1024
        ),
    )(nope, rope, ans.T, *rest)
    res = pl.pallas_call(
        hand_over,
        out_shape=outs,
        in_specs=[pl.BlockSpec(memory_space=pltpu.VMEM)] * 6,
        out_specs=(pl.BlockSpec(memory_space=pltpu.VMEM),) * 6,
    )(*got)
    return res[0], res[1], res[2].T, res[3], res[4], res[5]


def solution(mesh):
    return jax.shard_map(
        per_device,
        mesh=mesh,
        in_specs=(
            P("ans", "head"),
            P("ans", "head"),
            P("ans", None),
            P("ans", None),
            P("head", None, None),
            P("head", None, None),
            P("ans", "head"),
            P("ans"),
        ),
        out_specs=(
            P("ans", "head"),
            P("ans", "head"),
            P("ans", None),
            P("ans", None),
            P("head", "ans", None),
            P("head", "ans", None),
        ),
        check_vma=False,
    )
```

```python
import jax
import jax.numpy as jnp
from jax import lax
from jax.experimental import pallas as pl
from jax.experimental.pallas import tpu as pltpu
from jax.sharding import PartitionSpec as P

LAT = 512
ROPE = 64
HD = 128
VD = 128
GROUP = 64
W = LAT + ROPE
MESH = pl.DeviceIdType.MESH
F32 = jnp.float32
BF = jnp.bfloat16
SCALE = (HD + ROPE) ** (-0.5)
EXP2 = SCALE * 1.4426950408889634

T = 128
H = 8
R = T * H
SH = 96
KP = 1536
KA = KP + T
PAIR = 2 * T


def nn(a, b):
    return jnp.dot(a, b, preferred_element_type=F32)


def nt(a, b):
    return lax.dot_general(a, b, (((1,), (1,)), ((), ())), preferred_element_type=F32)


def kernel(
    nope_in, rope_in, ans_in, prm_in, wuk_in, wuv_in, gh_in, valid,
    o_nope, o_rope, o_ans, o_prm, o_wk, o_wv,
    nope, rope, wuk, wuv, gh, v_nope, v_rope, v_ans, v_prm, v_wk, v_wv,
    kall, kt, q, glt, glp, gl, s, gp, p, ds, mx, g,
    gs, gcr, xs, xr, zs, zr, fz, ag,
    as_, ar, fa, aa,
    wvt, wvs, wvc, wvacc, wvy, wvr, wvz, wvzs, wvzr,
    wkt, wks, wkc, wkacc, wky, wkr, wkz, wkzs, wkzr,
    sin, sout,
    sz, rz, sn, rn, sf, rf, scc, rcc,
    sgc, rgc, sxy, rxy, szz, rzz, sag, rag,
    sa1, ra1, sa2, ra2,
    swv, rwv, swk, rwk,
):
    h = lax.axis_index("head")
    a = lax.axis_index("ans")
    x, zl = h // 4, h % 4
    y, zh, c = a // 4, (a // 2) % 2, a % 2
    oc, ozh = 1 - c, 1 - zh
    hx = x % 2

    def dev(x_, y_, zh_, zl_, c_):
        return {"head": x_ * 4 + zl_, "ans": y_ * 4 + zh_ * 2 + c_}

    sib = dev(x, y, zh, zl, oc)

    def rc(src, dst, ss, rs, d):
        return pltpu.make_async_remote_copy(
            src_ref=src, dst_ref=dst, send_sem=ss, recv_sem=rs, device_id=d, device_id_type=MESH
        )

    def arrived(dst, rs):
        rc(dst, dst, rs, rs, sib).wait_recv()

    def sent(src, ss):
        rc(src, src, ss, ss, sib).wait_send()

    def yk(k):
        return (y + k) % 4

    partners = [dev((x + i) % 4, (y + j) % 4, zh, zl, c) for i in range(4) for j in range(4) if i + j > 0]
    partners += [dev((x + i) % 4, y, zh, (zl + j) % 4, c) for i in range(4) for j in range(1, 4)]
    partners += [dev(x, y, ozh, i, c) for i in range(4)] + [sib]
    bar = pltpu.get_barrier_semaphore()
    for d in partners:
        pl.semaphore_signal(bar, inc=1, device_id=d, device_id_type=MESH)

    def rows(y_, zh_, c_, half=None):
        base = zh_ * 768 + c_ * 384 + y_ * SH
        if half is None:
            return kall.at[pl.ds(pl.multiple_of(base, 16), SH)]
        return kall.at[pl.ds(pl.multiple_of(base + half * 48, 16), 48)]

    loads = [
        pltpu.make_async_copy(src, dst, sin.at[i])
        for i, (src, dst) in enumerate(
            [(prm_in, rows(y, zh, c)), (nope_in, nope), (rope_in, rope), (wuk_in, wuk), (wuv_in, wuv),
             (gh_in, gh), (ans_in, kt.at[:, pl.ds(KP, T)])]
        )
    ]
    for cp in loads:
        cp.start()
    for cp in loads:
        cp.wait()

    v0, v1 = valid[0], valid[1]
    tok = lax.broadcasted_iota(jnp.int32, (T, T), 0)
    live = (tok % GROUP < jnp.where(tok < GROUP, v0, v1)).astype(F32)

    def project(i, _):
        for hh in range(2):
            hd = 2 * i + hh
            lanes = pl.ds(pl.multiple_of(hd * T, T), T)
            qrows = pl.ds(pl.multiple_of(hd * T, T), T)
            q[qrows, :LAT] = nn(nope[:, lanes], wuk[hd]).astype(BF)
            pairs = rope[:, pl.ds(pl.multiple_of(i * 2 * ROPE, 2 * ROPE), 2 * ROPE)]
            q[qrows, LAT:] = pairs[:, hh * ROPE:(hh + 1) * ROPE]
            live_grad = (gh[:, lanes].astype(F32) * live).astype(BF)
            gl[:, lanes] = live_grad
            glt[:, lanes] = nt(wuv[hd], live_grad).astype(BF)
        return 0

    lax.fori_loop(0, H // 2, project, 0, unroll=True)
    pl.semaphore_wait(bar, len(partners))

    near_view = rows(y, zh, c, hx)
    far_view = rows(y, ozh, c, hx)
    xn = (x + 1 + 2 * c) % 4

    def near_copy(i, j):
        return rc(near_view, near_view, sn.at[i * 3 + j - 1], rn.at[i * 3 + 3 - j],
                  dev(xn if i else x, yk(j), zh, zl, c))

    def far_copy(i, j):
        return rc(far_view, far_view, sf.at[i * 4 + j], rf.at[i * 4 + (4 - j) % 4],
                  dev(xn if i else x, yk(j), zh, zl, c))

    near_all = [(1, 2), (0, 2), (1, 1), (1, 3), (0, 1), (0, 3)]
    far_all = near_all + [(1, 0)]

    def z_copy(to_zl, i):
        return rc(near_view, near_view, sz.at[i], rz.at[0], dev(x, y, ozh, to_zl, c))

    @pl.when(zl == 3)
    def _():
        z_copy(1, 1).start()
        z_copy(0, 0).start()

    @pl.when(zl == 0)
    def _():
        z_copy(2, 1).start()
        z_copy(3, 0).start()

    for i, j in near_all:
        near_copy(i, j).start()

    def c_send(zr_, r):
        view = rows(yk(r), zh if zr_ == 0 else ozh, c)
        return rc(view, view, scc.at[zr_ * 4 + r], rcc.at[zr_ * 4 + r], sib)

    def c_wait(zr_, r):
        arrived(rows(yk(r), zh if zr_ == 0 else ozh, oc), rcc.at[zr_ * 4 + r])

    c_send(0, 0).start()
    mx[...] = jnp.full_like(mx, -1e30)

    def scores(base, n, masked):
        def one(i, _):
            cols = pl.ds(pl.multiple_of(i * PAIR, PAIR), PAIR)
            sv = nt(kall[pl.ds(base, n), :], q[cols, :])
            if masked:
                j = lax.broadcasted_iota(jnp.int32, (n, PAIR), 0)
                t = lax.broadcasted_iota(jnp.int32, (n, PAIR), 1) % T
                lim = jnp.where(j < GROUP, v0, GROUP + v1)
                low = jnp.where(t < GROUP, 0, GROUP)
                sv = jnp.where((j <= t) & (j >= low) & (j < lim), sv, -1e30)
            s[pl.ds(base, n), cols] = sv
            mx[:, cols] = jnp.maximum(mx[:, cols], jnp.max(sv.reshape(n // 8, 8, PAIR), axis=0))
            gp[pl.ds(base, n), cols] = nn(kall[pl.ds(base, n), :LAT], glt[:, cols])
            return 0

        lax.fori_loop(0, R // PAIR, one, 0, unroll=True)

    def prompt_scores(base):
        base = pl.multiple_of(base, 128)
        kt[:, pl.ds(base, 384)] = kall[pl.ds(base, 384), :].T
        scores(base, 384, False)

    kall[KP:KA, :] = kt[:, KP:KA].T
    scores(KP, T, True)

    arrived(far_view, rz.at[0])
    for i, j in far_all:
        far_copy(i, j).start()
    for r in (1, 3, 2):
        for i in range(2):
            arrived(rows(yk(r), zh, c, 1 - hx if i else hx), rn.at[i * 3 + r - 1])
        c_send(0, r).start()
    prompt_scores(zh * 768 + c * 384)
    for r in range(4):
        c_wait(0, r)
    prompt_scores(zh * 768 + oc * 384)
    for r in (0, 1, 3, 2):
        for i in range(2):
            if i + r > 0:
                arrived(rows(yk(r), ozh, c, 1 - hx if i else hx), rf.at[i * 4 + r])
        c_send(1, r).start()
    prompt_scores(ozh * 768 + c * 384)
    for r in range(4):
        c_wait(1, r)
    prompt_scores(ozh * 768 + oc * 384)

    def wv_copy(i):
        return rc(wvs.at[i], wvc.at[i], swv.at[i], rwv.at[i], sib)

    def wk_copy(i):
        return rc(wks.at[i], wkc.at[i], swk.at[i], rwk.at[i], sib)

    def y_hop(i, k, buf, rbuf, ssem, rsem):
        n = 4 + 3 * i + k - 1
        return rc(buf.at[i, yk(k)], rbuf.at[i, k - 1], ssem.at[n], rsem.at[n], dev(x, yk(k), zh, zl, c))

    def z_hop(i, buf, rbuf, ssem, rsem):
        return rc(buf.at[i], rbuf.at[i], ssem.at[16 + i], rsem.at[16 + i], dev(x, y, ozh, zl, c))

    def wv_pair(i):
        wv_copy(i).wait_recv()
        t = wvacc[i] + wvc[i].astype(F32)
        wvacc[i] = t
        wvy[i] = t.astype(BF)
        for k in (2, 1, 3):
            y_hop(i, k, wvy, wvr, swv, rwv).start()

    def wk_pair(i):
        wk_copy(i).wait_recv()
        t = wkacc[i] + wkc[i].astype(F32)
        wkacc[i] = t
        wky[i] = t.astype(BF)
        for k in (2, 1, 3):
            y_hop(i, k, wky, wkr, swk, rwk).start()

    STEP = 128

    def softmax(i, _):
        cols = pl.ds(pl.multiple_of(i * PAIR, PAIR), PAIR)
        top = jnp.max(mx[:, cols], axis=0, keepdims=True)

        top = top * EXP2
        acc = jnp.zeros((8, PAIR), F32)
        for j in range(KA // STEP):
            rws = pl.ds(j * STEP, STEP)
            e = jnp.exp2(s[rws, cols] * EXP2 - top)
            s[rws, cols] = e
            low = e.astype(BF)
            p[rws, cols] = low
            acc = acc + jnp.sum(e.reshape(STEP // 8, 8, PAIR), axis=0)
        inv = 1.0 / jnp.sum(acc, axis=0, keepdims=True)
        lot = (nn(kt[:LAT, :], p[:, cols]) * inv).astype(BF)
        grad_latent = glt[:, cols].astype(F32)
        delta = jnp.sum(grad_latent * lot.astype(F32), axis=0, keepdims=True)
        glp[:, cols] = (grad_latent * inv).astype(BF)
        inv = inv * SCALE
        for j in range(KA // STEP):
            rws = pl.ds(j * STEP, STEP)
            ds[rws, cols] = (s[rws, cols] * inv * (gp[rws, cols] - delta)).astype(BF)
        for hh in range(2):
            lanes = pl.ds(pl.multiple_of((2 * i + hh) * T, T), T)
            wvt[...] = nn(lot[:, hh * T:(hh + 1) * T], gl[:, lanes]).reshape(8, 2, 32, VD)
            wvs[i, :, hh] = wvt[:, oc].reshape(4, 2, 32, VD).astype(BF)
            wvacc[i, :, hh] = wvt[:, c].reshape(4, 2, 32, VD)
        wv_copy(i).start()

        @pl.when(i > 0)
        def _():
            wv_pair(i - 1)

        return 0

    lax.fori_loop(0, R // PAIR, softmax, 0)

    def key_grad(base, n):
        rws = pl.ds(base, n)
        kq = nn(ds[rws, :], q[...])
        return kq[:, :LAT] + nt(p[rws, :], glp[...]), kq[:, LAT:]

    def owner_head(o):
        return (o // 2) * 4 + 1 + o % 2

    lat, rot = key_grad(KP, T)
    as_[:, :, :LAT] = lat.reshape(8, 16, LAT).astype(BF)
    as_[:, :, LAT:] = rot.reshape(8, 16, ROPE).astype(BF)
    wv_pair(3)
    for o in range(8):
        cp = rc(as_.at[o], ar.at[h], sa1.at[o], ra1.at[h], {"head": owner_head(o), "ans": a})

        @pl.when(h != owner_head(o))
        def _():
            cp.start()

    def gc_copy(i):
        return rc(gs.at[i], gcr.at[i], sgc.at[i], rgc.at[i], sib)

    def xy_copy(zz, yy, xx):
        n = zz * 16 + yy * 4 + xx
        m = zz * 16 + y * 4 + x
        return rc(xs.at[n], xr.at[m], sxy.at[n], rxy.at[m], dev(xx, yy, zh, zl, c))

    def to_owner(i, zz):
        for yy in range(4):
            sub = pl.ds(yy * SH, SH)
            t = g[sub, :] + gcr[i, sub, :].astype(F32)
            for xx in range(4):
                lat = t[:, xx * 128:(xx + 1) * 128]
                if xx < 3:
                    rot = t[32 * xx:32 * xx + 32, LAT:]
                    rot = jnp.concatenate([rot[:16], rot[16:]], axis=1)
                else:
                    rot = jnp.zeros((16, 128), F32)
                n = zz * 16 + yy * 4 + xx
                xs[n, :SH] = lat.astype(BF)
                xs[n, SH:] = rot.astype(BF)
        for j in (2, 1, 3, 0):
            for k in (2, 1, 3, 0):
                if j + k > 0:
                    xy_copy(zz, yk(j), (x + k) % 4).start()

    for i in range(2):
        zz = hx if i == 0 else 1 - hx
        lat, rot = key_grad(pl.multiple_of(zz * 768 + oc * 384, 128), 384)
        gs[i, :, :LAT] = lat.astype(BF)
        gs[i, :, LAT:] = rot.astype(BF)
        gc_copy(i).start()
        lat, rot = key_grad(pl.multiple_of(zz * 768 + c * 384, 128), 384)
        g[:, :LAT] = lat
        g[:, LAT:] = rot
        gc_copy(i).wait_recv()
        to_owner(i, zz)

    def wv_mid(i):
        for k in (1, 2, 3):
            y_hop(i, k, wvy, wvr, swv, rwv).wait_recv()
        t = wvacc[i, y]
        for k in (1, 2, 3):
            t = t + wvr[i, k - 1].astype(F32)
        wvz[i] = t
        wvzs[i] = wvz[i, :, ozh].astype(BF)
        z_hop(i, wvzs, wvzr, swv, rwv).start()

    def queries(i, _):
        cols = pl.ds(pl.multiple_of(i * PAIR, PAIR), PAIR)
        gqt = nn(kt[...], ds[:, cols])
        glq = gqt[:LAT].astype(BF)
        rot = gqt[LAT:].T
        for hh in range(2):
            hd = 2 * i + hh
            lanes = pl.ds(pl.multiple_of(hd * T, T), T)
            part = glq[:, hh * T:(hh + 1) * T]
            v_nope[:, lanes] = nn(wuk[hd], part).T.astype(BF)
            nope_t = nope[:, lanes].astype(F32).T.astype(BF)
            wkt[...] = nt(nope_t, part).reshape(8, 2, 8, LAT)
            wks[i, :, hh] = wkt[:, oc].reshape(4, 16, LAT).astype(BF)
            wkacc[i, :, hh] = wkt[:, c].reshape(4, 16, LAT)
        v_rope[:, pl.ds(pl.multiple_of(i * T, T), T)] = jnp.concatenate(
            [rot[:T], rot[T:]], axis=1).astype(BF)
        wk_copy(i).start()

        wv_mid(i)
        return 0

    lax.fori_loop(0, 4, queries, 0)
    out_nope = pltpu.make_async_copy(v_nope, o_nope, sout.at[0])
    out_rope = pltpu.make_async_copy(v_rope, o_rope, sout.at[1])
    out_nope.start()
    out_rope.start()

    for i in range(4):
        wk_pair(i)

    me_xy = y * 4 + x
    me_z = zh * 4 + zl

    def zz_copy(n):
        return rc(zs.at[n], zr.at[me_z], szz.at[n], rzz.at[me_z], dev(x, y, n // 4, n % 4, c))

    for zz in (hx, 1 - hx):
        for i in range(1, 16):
            src = zz * 16 + (me_xy + i) % 16
            arrived(xr.at[src], rxy.at[src])
        xr[zz * 16 + me_xy] = xs[zz * 16 + me_xy]
        acc = jnp.zeros((SH + 16, 128), F32)
        for i in range(16):
            acc = acc + xr[zz * 16 + i].astype(F32)
        acc = acc.astype(BF)
        for i in range(3):
            zs[zz * 4 + i] = acc[32 * i:32 * i + 32]
        zs[zz * 4 + 3, :16] = acc[SH:]
        zs[zz * 4 + 3, 16:] = jnp.zeros((16, 128), BF)
        for i in (2, 1, 3, 0):
            goal = zz * 4 + (zl + i) % 4

            @pl.when(me_z != goal)
            def _():
                zz_copy(goal).start()

    is_owner = (zl == 1) | (zl == 2)
    mine = x * 2 + zl - 1

    def answer_out(i):
        return rc(fa, aa.at[mine], sa2.at[i - 1], ra2.at[mine], {"head": (h + i) % 16, "ans": a})

    @pl.when(is_owner)
    def _():
        ar[h] = as_[mine]
        for i in range(1, 16):
            src = (h + i) % 16
            arrived(ar.at[src], ra1.at[src])
        acc = jnp.zeros((16, W), F32)
        for i in range(16):
            acc = acc + ar[i].astype(F32)
        fa[...] = acc.astype(BF)
        for i in range(1, 16):
            answer_out(i).start()
        aa[mine] = fa[...]

    def ag_copy(i):
        return rc(fz, ag.at[h], sag.at[i - 1], rag.at[h], {"head": (h + i) % 16, "ans": a})

    zr[me_z] = zs[me_z]
    for i in range(1, 8):
        src = (me_z + i) % 8
        arrived(zr.at[src], rzz.at[src])
    tot = jnp.zeros((32, 128), F32)
    for i in range(8):
        tot = tot + zr[i].astype(F32)
    fz[...] = tot.astype(BF)
    for i in range(1, 16):
        ag_copy(i).start()
    ag[h] = fz[...]

    def wk_mid(i, _):
        for k in (1, 2, 3):
            y_hop(i, k, wky, wkr, swk, rwk).wait_recv()
        t = wkacc[i, y]
        for k in (1, 2, 3):
            t = t + wkr[i, k - 1].astype(F32)
        wkz[i] = t.reshape(2, 2, 8, LAT)
        wkzs[i] = wkz[i, :, ozh].reshape(16, LAT).astype(BF)
        z_hop(i, wkzs, wkzr, swk, rwk).start()
        return 0

    lax.fori_loop(0, 4, wk_mid, 0)

    for o in range(8):
        @pl.when(h != owner_head(o))
        def _():
            arrived(aa.at[o], ra2.at[o])

    v_ans[...] = aa[...].astype(F32).reshape(T, W).T
    out_ans = pltpu.make_async_copy(v_ans, o_ans, sout.at[2])
    out_ans.start()

    def weights_out(i, _):
        z_hop(i, wvzs, wvzr, swv, rwv).wait_recv()
        v_wv[pl.ds(2 * i, 2)] = wvz[i, :, zh] + wvzr[i].astype(F32)
        z_hop(i, wkzs, wkzr, swk, rwk).wait_recv()
        v_wk[pl.ds(2 * i, 2)] = wkz[i, :, zh] + wkzr[i].astype(F32).reshape(2, 8, LAT)
        return 0

    lax.fori_loop(0, 4, weights_out, 0)
    out_wk = pltpu.make_async_copy(v_wk, o_wk, sout.at[3])
    out_wv = pltpu.make_async_copy(v_wv, o_wv, sout.at[4])
    out_wk.start()
    out_wv.start()

    for zr_ in range(2):
        for r in range(4):
            c_send(zr_, r).wait_send()

    for i, j in near_all:
        near_copy(i, j).wait_send()
    for i, j in far_all:
        far_copy(i, j).wait_send()

    @pl.when((zl == 3) | (zl == 0))
    def _():
        sent(near_view, sz.at[0])
        sent(near_view, sz.at[1])

    for o in range(8):
        @pl.when(h != owner_head(o))
        def _():
            sent(as_.at[o], sa1.at[o])

    @pl.when(is_owner)
    def _():
        for i in range(1, 16):
            sent(fa, sa2.at[i - 1])

    for i in range(8):
        @pl.when(me_z != i)
        def _():
            sent(zs.at[i], szz.at[i])

    for zz in range(2):
        for i in range(1, 16):
            dst = zz * 16 + (me_xy + i) % 16
            sent(xs.at[dst], sxy.at[dst])

    for i in range(2):
        gc_copy(i).wait_send()

    def drain(i, _):
        wv_copy(i).wait_send()
        wk_copy(i).wait_send()
        for k in (1, 2, 3):
            y_hop(i, k, wvy, wvr, swv, rwv).wait_send()
            y_hop(i, k, wky, wkr, swk, rwk).wait_send()
        z_hop(i, wvzs, wvzr, swv, rwv).wait_send()
        z_hop(i, wkzs, wkzr, swk, rwk).wait_send()
        return 0

    lax.fori_loop(0, 4, drain, 0)

    for i in range(1, 16):
        src = (h + i) % 16
        arrived(ag.at[src], rag.at[src])

    for xx in range(4):
        for i in range(3):
            v_prm[32 * i:32 * i + 32, 128 * xx:128 * xx + 128] = ag[xx * 4 + i].astype(F32)
        if xx < 3:
            rot = ag[xx * 4 + 3].astype(F32)
            v_prm[32 * xx:32 * xx + 16, LAT:] = rot[:16, :ROPE]
            v_prm[32 * xx + 16:32 * xx + 32, LAT:] = rot[:16, ROPE:]
    out_prm = pltpu.make_async_copy(v_prm, o_prm, sout.at[5])
    out_prm.start()

    for i in range(1, 16):
        sent(fz, sag.at[i - 1])

    for cp in (out_nope, out_rope, out_ans, out_wk, out_wv, out_prm):
        cp.wait()


def hand_over(*refs):
    held, sem_in, sem_out = refs[12:18], refs[18], refs[19]
    loads = [pltpu.make_async_copy(refs[i], held[i], sem_in.at[i]) for i in range(6)]
    stores = [pltpu.make_async_copy(held[i], refs[6 + i], sem_out.at[i]) for i in range(6)]
    for cp in loads:
        cp.start()
    for i in range(6):
        loads[i].wait()
        stores[i].start()
    for cp in stores:
        cp.wait()


def per_device(nope, rope, ans, *rest):
    V = pltpu.VMEM
    D = pltpu.SemaphoreType.DMA
    outs = (
        jax.ShapeDtypeStruct((T, H * HD), BF),
        jax.ShapeDtypeStruct((T, H * ROPE), BF),
        jax.ShapeDtypeStruct((W, T), F32),
        jax.ShapeDtypeStruct((SH, W), F32),
        jax.ShapeDtypeStruct((H, 8, LAT), F32),
        jax.ShapeDtypeStruct((H, 32, VD), F32),
    )
    scratch = [
        V((T, H * HD), BF), V((T, H * ROPE), BF), V((H, HD, LAT), BF), V((H, LAT, VD), BF), V((T, H * VD), BF),
    ] + [V(o.shape, o.dtype) for o in outs] + [
        V((KA, W), BF), V((W, KA), BF), V((R, W), BF), V((LAT, R), BF), V((LAT, R), BF), V((T, H * VD), BF),
        V((KA, R), F32), V((KA, R), F32), V((KA, R), BF), V((KA, R), BF), V((8, R), F32), V((384, W), F32),
        V((2, 384, W), BF), V((2, 384, W), BF), V((32, SH + 16, 128), BF), V((32, SH + 16, 128), BF),
        V((8, 32, 128), BF), V((8, 32, 128), BF), V((32, 128), BF), V((16, 32, 128), BF),
        V((8, 16, W), BF), V((16, 16, W), BF), V((16, W), BF), V((8, 16, W), BF),
        V((8, 2, 32, VD), F32), V((4, 4, 2, 2, 32, VD), BF), V((4, 4, 2, 2, 32, VD), BF),
        V((4, 4, 2, 2, 32, VD), F32), V((4, 4, 2, 2, 32, VD), BF), V((4, 3, 2, 2, 32, VD), BF),
        V((4, 2, 2, 32, VD), F32), V((4, 2, 32, VD), BF), V((4, 2, 32, VD), BF),
        V((8, 2, 8, LAT), F32), V((4, 4, 2, 16, LAT), BF), V((4, 4, 2, 16, LAT), BF),
        V((4, 4, 2, 16, LAT), F32), V((4, 4, 2, 16, LAT), BF), V((4, 3, 2, 16, LAT), BF),
        V((4, 2, 2, 8, LAT), F32), V((4, 16, LAT), BF), V((4, 16, LAT), BF),
        D((7,)), D((6,)),
        D((2,)), D((1,)), D((6,)), D((6,)), D((8,)), D((8,)), D((8,)), D((8,)),
        D((2,)), D((2,)), D((32,)), D((32,)), D((8,)), D((8,)), D((15,)), D((16,)),
        D((8,)), D((16,)), D((15,)), D((8,)),
        D((20,)), D((20,)), D((20,)), D((20,)),
    ]
    hbm = pl.BlockSpec(memory_space=pl.ANY)
    got = pl.pallas_call(
        kernel,
        out_shape=outs,
        in_specs=[hbm] * 7 + [pl.BlockSpec(memory_space=pltpu.SMEM)],
        out_specs=(hbm,) * 6,
        scratch_shapes=scratch,
        compiler_params=pltpu.CompilerParams(
            collective_id=0, has_side_effects=True, vmem_limit_bytes=62 * 1024 * 1024
        ),
    )(nope, rope, ans.T, *rest)
    res = pl.pallas_call(
        hand_over,
        out_shape=outs,
        in_specs=[hbm] * 6,
        out_specs=(hbm,) * 6,
        scratch_shapes=[V(o.shape, o.dtype) for o in outs] + [D((6,)), D((6,))],
    )(*got)
    return res[0], res[1], res[2].T, res[3], res[4], res[5]


def solution(mesh):
    return jax.shard_map(
        per_device,
        mesh=mesh,
        in_specs=(
            P("ans", "head"),
            P("ans", "head"),
            P("ans", None),
            P("ans", None),
            P("head", None, None),
            P("head", None, None),
            P("ans", "head"),
            P("ans"),
        ),
        out_specs=(
            P("ans", "head"),
            P("ans", "head"),
            P("ans", None),
            P("ans", None),
            P("head", "ans", None),
            P("head", "ans", None),
        ),
        check_vma=False,
    )
```

```python
import jax
import jax.numpy as jnp
from jax import lax
from jax.experimental import pallas as pl
from jax.experimental.pallas import tpu as pltpu
from jax.sharding import PartitionSpec as P

LAT = 512
ROPE = 64
HD = 128
VD = 128
GROUP = 64
W = LAT + ROPE
MESH = pl.DeviceIdType.MESH
F32 = jnp.float32
BF = jnp.bfloat16
SCALE = (HD + ROPE) ** (-0.5)
EXP2 = SCALE * 1.4426950408889634

T = 128
H = 8
R = T * H
SH = 96
KP = 1536
KA = KP + T
PAIR = 2 * T


def nn(a, b):
    return jnp.dot(a, b, preferred_element_type=F32)


def nt(a, b):
    return lax.dot_general(a, b, (((1,), (1,)), ((), ())), preferred_element_type=F32)


def kernel(
    nope_in, rope_in, ans_in, prm_in, wuk_in, wuv_in, gh_in, valid,
    o_nope, o_rope, o_ans, o_prm, o_wk, o_wv,
    nope, rope, wuk, wuv, gh, v_nope, v_rope, v_ans, v_prm, v_wk, v_wv,
    kall, kt, q, glt, glp, gl, s, gp, p, ds, mx, g,
    gs, gcr, xs, xr, zs, zr, fz, ag,
    as_, ar, fa, aa,
    wvt, wvs, wvc, wvacc, wvy, wvr, wvz, wvzs, wvzr,
    wkt, wks, wkc, wkacc, wky, wkr, wkz, wkzs, wkzr,
    sin, sout,
    sz, rz, sn, rn, sf, rf, scc, rcc,
    sgc, rgc, sxy, rxy, szz, rzz, sag, rag,
    sa1, ra1, sa2, ra2,
    swv, rwv, swk, rwk,
):
    h = lax.axis_index("head")
    a = lax.axis_index("ans")
    x, zl = h // 4, h % 4
    y, zh, c = a // 4, (a // 2) % 2, a % 2
    oc, ozh = 1 - c, 1 - zh
    hx = x % 2

    def dev(x_, y_, zh_, zl_, c_):
        return {"head": x_ * 4 + zl_, "ans": y_ * 4 + zh_ * 2 + c_}

    sib = dev(x, y, zh, zl, oc)

    def rc(src, dst, ss, rs, d):
        return pltpu.make_async_remote_copy(
            src_ref=src, dst_ref=dst, send_sem=ss, recv_sem=rs, device_id=d, device_id_type=MESH
        )

    def arrived(dst, rs):
        rc(dst, dst, rs, rs, sib).wait_recv()

    def sent(src, ss):
        rc(src, src, ss, ss, sib).wait_send()

    def yk(k):
        return (y + k) % 4

    partners = [dev((x + i) % 4, (y + j) % 4, zh, zl, c) for i in range(4) for j in range(4) if i + j > 0]
    partners += [dev((x + i) % 4, y, zh, (zl + j) % 4, c) for i in range(4) for j in range(1, 4)]
    partners += [dev(x, y, ozh, i, c) for i in range(4)] + [sib]
    bar = pltpu.get_barrier_semaphore()
    for d in partners:
        pl.semaphore_signal(bar, inc=1, device_id=d, device_id_type=MESH)

    def rows(y_, zh_, c_, half=None):
        base = zh_ * 768 + c_ * 384 + y_ * SH
        if half is None:
            return kall.at[pl.ds(pl.multiple_of(base, 16), SH)]
        return kall.at[pl.ds(pl.multiple_of(base + half * 48, 16), 48)]

    loads = [
        pltpu.make_async_copy(src, dst, sin.at[i])
        for i, (src, dst) in enumerate(
            [(prm_in, rows(y, zh, c)), (nope_in, nope), (rope_in, rope), (wuk_in, wuk), (wuv_in, wuv),
             (gh_in, gh), (ans_in, kt.at[:, pl.ds(KP, T)])]
        )
    ]
    for cp in loads:
        cp.start()
    for cp in loads:
        cp.wait()

    v0, v1 = valid[0], valid[1]
    tok = lax.broadcasted_iota(jnp.int32, (T, T), 0)
    live = (tok % GROUP < jnp.where(tok < GROUP, v0, v1)).astype(F32)

    def project(i, _):
        for hh in range(2):
            hd = 2 * i + hh
            lanes = pl.ds(pl.multiple_of(hd * T, T), T)
            qrows = pl.ds(pl.multiple_of(hd * T, T), T)
            q[qrows, :LAT] = nn(nope[:, lanes], wuk[hd]).astype(BF)
            pairs = rope[:, pl.ds(pl.multiple_of(i * 2 * ROPE, 2 * ROPE), 2 * ROPE)]
            q[qrows, LAT:] = pairs[:, hh * ROPE:(hh + 1) * ROPE]
            live_grad = (gh[:, lanes].astype(F32) * live).astype(BF)
            gl[:, lanes] = live_grad
            glt[:, lanes] = nt(wuv[hd], live_grad).astype(BF)
        return 0

    lax.fori_loop(0, H // 2, project, 0, unroll=True)
    pl.semaphore_wait(bar, len(partners))

    near_view = rows(y, zh, c, hx)
    far_view = rows(y, ozh, c, hx)
    xn = (x + 1 + 2 * c) % 4

    def near_copy(i, j):
        return rc(near_view, near_view, sn.at[i * 3 + j - 1], rn.at[i * 3 + 3 - j],
                  dev(xn if i else x, yk(j), zh, zl, c))

    def far_copy(i, j):
        return rc(far_view, far_view, sf.at[i * 4 + j], rf.at[i * 4 + (4 - j) % 4],
                  dev(xn if i else x, yk(j), zh, zl, c))

    near_all = [(1, 2), (0, 2), (1, 1), (1, 3), (0, 1), (0, 3)]
    far_all = near_all + [(1, 0)]

    def z_copy(to_zl, i):
        return rc(near_view, near_view, sz.at[i], rz.at[0], dev(x, y, ozh, to_zl, c))

    @pl.when(zl == 3)
    def _():
        z_copy(1, 1).start()
        z_copy(0, 0).start()

    @pl.when(zl == 0)
    def _():
        z_copy(2, 1).start()
        z_copy(3, 0).start()

    for i, j in near_all:
        near_copy(i, j).start()

    def c_send(zr_, r):
        view = rows(yk(r), zh if zr_ == 0 else ozh, c)
        return rc(view, view, scc.at[zr_ * 4 + r], rcc.at[zr_ * 4 + r], sib)

    def c_wait(zr_, r):
        arrived(rows(yk(r), zh if zr_ == 0 else ozh, oc), rcc.at[zr_ * 4 + r])

    c_send(0, 0).start()
    mx[...] = jnp.full_like(mx, -1e30)

    def scores(base, n, masked):
        def one(i, _):
            cols = pl.ds(pl.multiple_of(i * PAIR, PAIR), PAIR)
            sv = nt(kall[pl.ds(base, n), :], q[cols, :])
            if masked:
                j = lax.broadcasted_iota(jnp.int32, (n, PAIR), 0)
                t = lax.broadcasted_iota(jnp.int32, (n, PAIR), 1) % T
                lim = jnp.where(j < GROUP, v0, GROUP + v1)
                low = jnp.where(t < GROUP, 0, GROUP)
                sv = jnp.where((j <= t) & (j >= low) & (j < lim), sv, -1e30)
            s[pl.ds(base, n), cols] = sv
            mx[:, cols] = jnp.maximum(mx[:, cols], jnp.max(sv.reshape(n // 8, 8, PAIR), axis=0))
            gp[pl.ds(base, n), cols] = nn(kall[pl.ds(base, n), :LAT], glt[:, cols])
            return 0

        lax.fori_loop(0, R // PAIR, one, 0, unroll=True)

    def prompt_scores(base):
        base = pl.multiple_of(base, 128)
        kt[:, pl.ds(base, 384)] = kall[pl.ds(base, 384), :].T
        scores(base, 384, False)

    kall[KP:KA, :] = kt[:, KP:KA].T
    scores(KP, T, True)

    arrived(far_view, rz.at[0])
    for i, j in far_all:
        far_copy(i, j).start()
    for r in (1, 3, 2):
        for i in range(2):
            arrived(rows(yk(r), zh, c, 1 - hx if i else hx), rn.at[i * 3 + r - 1])
        c_send(0, r).start()
    prompt_scores(zh * 768 + c * 384)
    for r in range(4):
        c_wait(0, r)
    prompt_scores(zh * 768 + oc * 384)
    for r in (0, 1, 3, 2):
        for i in range(2):
            if i + r > 0:
                arrived(rows(yk(r), ozh, c, 1 - hx if i else hx), rf.at[i * 4 + r])
        c_send(1, r).start()
    prompt_scores(ozh * 768 + c * 384)
    for r in range(4):
        c_wait(1, r)
    prompt_scores(ozh * 768 + oc * 384)

    def wv_copy(i):
        return rc(wvs.at[i], wvc.at[i], swv.at[i], rwv.at[i], sib)

    def wk_copy(i):
        return rc(wks.at[i], wkc.at[i], swk.at[i], rwk.at[i], sib)

    def y_hop(i, k, buf, rbuf, ssem, rsem):
        n = 4 + 3 * i + k - 1
        return rc(buf.at[i, yk(k)], rbuf.at[i, k - 1], ssem.at[n], rsem.at[n], dev(x, yk(k), zh, zl, c))

    def z_hop(i, buf, rbuf, ssem, rsem):
        return rc(buf.at[i], rbuf.at[i], ssem.at[16 + i], rsem.at[16 + i], dev(x, y, ozh, zl, c))

    def wv_pair(i):
        wv_copy(i).wait_recv()
        t = wvacc[i] + wvc[i].astype(F32)
        wvacc[i] = t
        wvy[i] = t.astype(BF)
        for k in (2, 1, 3):
            y_hop(i, k, wvy, wvr, swv, rwv).start()

    def wk_pair(i):
        wk_copy(i).wait_recv()
        t = wkacc[i] + wkc[i].astype(F32)
        wkacc[i] = t
        wky[i] = t.astype(BF)
        for k in (2, 1, 3):
            y_hop(i, k, wky, wkr, swk, rwk).start()

    STEP = 128

    def softmax(i, _):
        cols = pl.ds(pl.multiple_of(i * PAIR, PAIR), PAIR)
        top = jnp.max(mx[:, cols], axis=0, keepdims=True)

        top = top * EXP2
        acc = jnp.zeros((8, PAIR), F32)
        for j in range(KA // STEP):
            rws = pl.ds(j * STEP, STEP)
            e = jnp.exp2(s[rws, cols] * EXP2 - top)
            s[rws, cols] = e
            low = e.astype(BF)
            p[rws, cols] = low
            acc = acc + jnp.sum(e.reshape(STEP // 8, 8, PAIR), axis=0)
        inv = 1.0 / jnp.sum(acc, axis=0, keepdims=True)
        lot = (nn(kt[:LAT, :], p[:, cols]) * inv).astype(BF)
        grad_latent = glt[:, cols].astype(F32)
        delta = jnp.sum(grad_latent * lot.astype(F32), axis=0, keepdims=True)
        glp[:, cols] = (grad_latent * inv).astype(BF)
        inv = inv * SCALE
        for j in range(KA // STEP):
            rws = pl.ds(j * STEP, STEP)
            ds[rws, cols] = (s[rws, cols] * inv * (gp[rws, cols] - delta)).astype(BF)
        for hh in range(2):
            lanes = pl.ds(pl.multiple_of((2 * i + hh) * T, T), T)
            wvt[...] = nn(lot[:, hh * T:(hh + 1) * T], gl[:, lanes]).reshape(8, 2, 32, VD)
            wvs[i, :, hh] = wvt[:, oc].reshape(4, 2, 32, VD).astype(BF)
            wvacc[i, :, hh] = wvt[:, c].reshape(4, 2, 32, VD)
        wv_copy(i).start()

        @pl.when(i > 0)
        def _():
            wv_pair(i - 1)

        return 0

    lax.fori_loop(0, R // PAIR, softmax, 0)

    def key_grad(base, n):
        rws = pl.ds(base, n)
        kq = nn(ds[rws, :], q[...])
        return kq[:, :LAT] + nt(p[rws, :], glp[...]), kq[:, LAT:]

    def owner_head(o):
        return (o // 2) * 4 + 1 + o % 2

    lat, rot = key_grad(KP, T)
    as_[:, :, :LAT] = lat.reshape(8, 16, LAT).astype(BF)
    as_[:, :, LAT:] = rot.reshape(8, 16, ROPE).astype(BF)
    wv_pair(3)
    for o in range(8):
        cp = rc(as_.at[o], ar.at[h], sa1.at[o], ra1.at[h], {"head": owner_head(o), "ans": a})

        @pl.when(h != owner_head(o))
        def _():
            cp.start()

    def gc_copy(i):
        return rc(gs.at[i], gcr.at[i], sgc.at[i], rgc.at[i], sib)

    def xy_copy(zz, yy, xx):
        n = zz * 16 + yy * 4 + xx
        m = zz * 16 + y * 4 + x
        return rc(xs.at[n], xr.at[m], sxy.at[n], rxy.at[m], dev(xx, yy, zh, zl, c))

    def to_owner(i, zz):
        for yy in range(4):
            sub = pl.ds(yy * SH, SH)
            t = g[sub, :] + gcr[i, sub, :].astype(F32)
            for xx in range(4):
                lat = t[:, xx * 128:(xx + 1) * 128]
                if xx < 3:
                    rot = t[32 * xx:32 * xx + 32, LAT:]
                    rot = jnp.concatenate([rot[:16], rot[16:]], axis=1)
                else:
                    rot = jnp.zeros((16, 128), F32)
                n = zz * 16 + yy * 4 + xx
                xs[n, :SH] = lat.astype(BF)
                xs[n, SH:] = rot.astype(BF)
        for j in (2, 1, 3, 0):
            for k in (2, 1, 3, 0):
                if j + k > 0:
                    xy_copy(zz, yk(j), (x + k) % 4).start()

    for i in range(2):
        zz = hx if i == 0 else 1 - hx
        lat, rot = key_grad(pl.multiple_of(zz * 768 + oc * 384, 128), 384)
        gs[i, :, :LAT] = lat.astype(BF)
        gs[i, :, LAT:] = rot.astype(BF)
        gc_copy(i).start()
        lat, rot = key_grad(pl.multiple_of(zz * 768 + c * 384, 128), 384)
        g[:, :LAT] = lat
        g[:, LAT:] = rot
        gc_copy(i).wait_recv()
        to_owner(i, zz)

    def wv_mid(i):
        for k in (1, 2, 3):
            y_hop(i, k, wvy, wvr, swv, rwv).wait_recv()
        t = wvacc[i, y]
        for k in (1, 2, 3):
            t = t + wvr[i, k - 1].astype(F32)
        wvz[i] = t
        wvzs[i] = wvz[i, :, ozh].astype(BF)
        z_hop(i, wvzs, wvzr, swv, rwv).start()

    def queries(i, _):
        cols = pl.ds(pl.multiple_of(i * PAIR, PAIR), PAIR)
        gqt = nn(kt[...], ds[:, cols])
        glq = gqt[:LAT].astype(BF)
        for hh in range(2):
            hd = 2 * i + hh
            lanes = pl.ds(pl.multiple_of(hd * T, T), T)
            part = glq[:, hh * T:(hh + 1) * T]
            nope_t = nope[:, lanes].astype(F32).T.astype(BF)
            wkt[...] = nt(nope_t, part).reshape(8, 2, 8, LAT)
            wks[i, :, hh] = wkt[:, oc].reshape(4, 16, LAT).astype(BF)
            wkacc[i, :, hh] = wkt[:, c].reshape(4, 16, LAT)
        wk_copy(i).start()
        for hh in range(2):
            hd = 2 * i + hh
            lanes = pl.ds(pl.multiple_of(hd * T, T), T)
            v_nope[:, lanes] = nn(wuk[hd], glq[:, hh * T:(hh + 1) * T]).T.astype(BF)
        rot = gqt[LAT:].T
        v_rope[:, pl.ds(pl.multiple_of(i * T, T), T)] = jnp.concatenate(
            [rot[:T], rot[T:]], axis=1).astype(BF)

        wv_mid(i)
        return 0

    lax.fori_loop(0, 4, queries, 0)
    out_nope = pltpu.make_async_copy(v_nope, o_nope, sout.at[0])
    out_rope = pltpu.make_async_copy(v_rope, o_rope, sout.at[1])
    out_nope.start()
    out_rope.start()

    for i in range(4):
        wk_pair(i)

    me_xy = y * 4 + x
    me_z = zh * 4 + zl

    def zz_copy(n):
        return rc(zs.at[n], zr.at[me_z], szz.at[n], rzz.at[me_z], dev(x, y, n // 4, n % 4, c))

    for zz in (hx, 1 - hx):
        for i in range(1, 16):
            src = zz * 16 + (me_xy + i) % 16
            arrived(xr.at[src], rxy.at[src])
        xr[zz * 16 + me_xy] = xs[zz * 16 + me_xy]
        acc = jnp.zeros((SH + 16, 128), F32)
        for i in range(16):
            acc = acc + xr[zz * 16 + i].astype(F32)
        acc = acc.astype(BF)
        for i in range(3):
            zs[zz * 4 + i] = acc[32 * i:32 * i + 32]
        zs[zz * 4 + 3, :16] = acc[SH:]
        zs[zz * 4 + 3, 16:] = jnp.zeros((16, 128), BF)
        for i in (2, 1, 3, 0):
            goal = zz * 4 + (zl + i) % 4

            @pl.when(me_z != goal)
            def _():
                zz_copy(goal).start()

    is_owner = (zl == 1) | (zl == 2)
    mine = x * 2 + zl - 1

    def answer_out(i):
        return rc(fa, aa.at[mine], sa2.at[i - 1], ra2.at[mine], {"head": (h + i) % 16, "ans": a})

    @pl.when(is_owner)
    def _():
        ar[h] = as_[mine]
        for i in range(1, 16):
            src = (h + i) % 16
            arrived(ar.at[src], ra1.at[src])
        acc = jnp.zeros((16, W), F32)
        for i in range(16):
            acc = acc + ar[i].astype(F32)
        fa[...] = acc.astype(BF)
        for i in range(1, 16):
            answer_out(i).start()
        aa[mine] = fa[...]

    def ag_copy(i):
        return rc(fz, ag.at[h], sag.at[i - 1], rag.at[h], {"head": (h + i) % 16, "ans": a})

    zr[me_z] = zs[me_z]
    for i in range(1, 8):
        src = (me_z + i) % 8
        arrived(zr.at[src], rzz.at[src])
    tot = jnp.zeros((32, 128), F32)
    for i in range(8):
        tot = tot + zr[i].astype(F32)
    fz[...] = tot.astype(BF)
    for i in range(1, 16):
        ag_copy(i).start()
    ag[h] = fz[...]

    def wk_mid(i, _):
        for k in (1, 2, 3):
            y_hop(i, k, wky, wkr, swk, rwk).wait_recv()
        t = wkacc[i, y]
        for k in (1, 2, 3):
            t = t + wkr[i, k - 1].astype(F32)
        wkz[i] = t.reshape(2, 2, 8, LAT)
        wkzs[i] = wkz[i, :, ozh].reshape(16, LAT).astype(BF)
        z_hop(i, wkzs, wkzr, swk, rwk).start()
        return 0

    lax.fori_loop(0, 4, wk_mid, 0)

    for o in range(8):
        @pl.when(h != owner_head(o))
        def _():
            arrived(aa.at[o], ra2.at[o])

    v_ans[...] = aa[...].astype(F32).reshape(T, W).T
    out_ans = pltpu.make_async_copy(v_ans, o_ans, sout.at[2])
    out_ans.start()

    def weights_out(i, _):
        z_hop(i, wvzs, wvzr, swv, rwv).wait_recv()
        v_wv[pl.ds(2 * i, 2)] = wvz[i, :, zh] + wvzr[i].astype(F32)
        z_hop(i, wkzs, wkzr, swk, rwk).wait_recv()
        v_wk[pl.ds(2 * i, 2)] = wkz[i, :, zh] + wkzr[i].astype(F32).reshape(2, 8, LAT)
        return 0

    lax.fori_loop(0, 4, weights_out, 0)
    out_wk = pltpu.make_async_copy(v_wk, o_wk, sout.at[3])
    out_wv = pltpu.make_async_copy(v_wv, o_wv, sout.at[4])
    out_wk.start()
    out_wv.start()

    for zr_ in range(2):
        for r in range(4):
            c_send(zr_, r).wait_send()

    for i, j in near_all:
        near_copy(i, j).wait_send()
    for i, j in far_all:
        far_copy(i, j).wait_send()

    @pl.when((zl == 3) | (zl == 0))
    def _():
        sent(near_view, sz.at[0])
        sent(near_view, sz.at[1])

    for o in range(8):
        @pl.when(h != owner_head(o))
        def _():
            sent(as_.at[o], sa1.at[o])

    @pl.when(is_owner)
    def _():
        for i in range(1, 16):
            sent(fa, sa2.at[i - 1])

    for i in range(8):
        @pl.when(me_z != i)
        def _():
            sent(zs.at[i], szz.at[i])

    for zz in range(2):
        for i in range(1, 16):
            dst = zz * 16 + (me_xy + i) % 16
            sent(xs.at[dst], sxy.at[dst])

    for i in range(2):
        gc_copy(i).wait_send()

    def drain(i, _):
        wv_copy(i).wait_send()
        wk_copy(i).wait_send()
        for k in (1, 2, 3):
            y_hop(i, k, wvy, wvr, swv, rwv).wait_send()
            y_hop(i, k, wky, wkr, swk, rwk).wait_send()
        z_hop(i, wvzs, wvzr, swv, rwv).wait_send()
        z_hop(i, wkzs, wkzr, swk, rwk).wait_send()
        return 0

    lax.fori_loop(0, 4, drain, 0)

    for i in range(1, 16):
        src = (h + i) % 16
        arrived(ag.at[src], rag.at[src])

    for xx in range(4):
        for i in range(3):
            v_prm[32 * i:32 * i + 32, 128 * xx:128 * xx + 128] = ag[xx * 4 + i].astype(F32)
        if xx < 3:
            rot = ag[xx * 4 + 3].astype(F32)
            v_prm[32 * xx:32 * xx + 16, LAT:] = rot[:16, :ROPE]
            v_prm[32 * xx + 16:32 * xx + 32, LAT:] = rot[:16, ROPE:]
    out_prm = pltpu.make_async_copy(v_prm, o_prm, sout.at[5])
    out_prm.start()

    for i in range(1, 16):
        sent(fz, sag.at[i - 1])

    for cp in (out_nope, out_rope, out_ans, out_wk, out_wv, out_prm):
        cp.wait()


def hand_over(*refs):
    held, sem_in, sem_out = refs[12:18], refs[18], refs[19]
    loads = [pltpu.make_async_copy(refs[i], held[i], sem_in.at[i]) for i in range(6)]
    stores = [pltpu.make_async_copy(held[i], refs[6 + i], sem_out.at[i]) for i in range(6)]
    for cp in loads:
        cp.start()
    for i in range(6):
        loads[i].wait()
        stores[i].start()
    for cp in stores:
        cp.wait()


def per_device(nope, rope, ans, *rest):
    V = pltpu.VMEM
    D = pltpu.SemaphoreType.DMA
    outs = (
        jax.ShapeDtypeStruct((T, H * HD), BF),
        jax.ShapeDtypeStruct((T, H * ROPE), BF),
        jax.ShapeDtypeStruct((W, T), F32),
        jax.ShapeDtypeStruct((SH, W), F32),
        jax.ShapeDtypeStruct((H, 8, LAT), F32),
        jax.ShapeDtypeStruct((H, 32, VD), F32),
    )
    scratch = [
        V((T, H * HD), BF), V((T, H * ROPE), BF), V((H, HD, LAT), BF), V((H, LAT, VD), BF), V((T, H * VD), BF),
    ] + [V(o.shape, o.dtype) for o in outs] + [
        V((KA, W), BF), V((W, KA), BF), V((R, W), BF), V((LAT, R), BF), V((LAT, R), BF), V((T, H * VD), BF),
        V((KA, R), F32), V((KA, R), F32), V((KA, R), BF), V((KA, R), BF), V((8, R), F32), V((384, W), F32),
        V((2, 384, W), BF), V((2, 384, W), BF), V((32, SH + 16, 128), BF), V((32, SH + 16, 128), BF),
        V((8, 32, 128), BF), V((8, 32, 128), BF), V((32, 128), BF), V((16, 32, 128), BF),
        V((8, 16, W), BF), V((16, 16, W), BF), V((16, W), BF), V((8, 16, W), BF),
        V((8, 2, 32, VD), F32), V((4, 4, 2, 2, 32, VD), BF), V((4, 4, 2, 2, 32, VD), BF),
        V((4, 4, 2, 2, 32, VD), F32), V((4, 4, 2, 2, 32, VD), BF), V((4, 3, 2, 2, 32, VD), BF),
        V((4, 2, 2, 32, VD), F32), V((4, 2, 32, VD), BF), V((4, 2, 32, VD), BF),
        V((8, 2, 8, LAT), F32), V((4, 4, 2, 16, LAT), BF), V((4, 4, 2, 16, LAT), BF),
        V((4, 4, 2, 16, LAT), F32), V((4, 4, 2, 16, LAT), BF), V((4, 3, 2, 16, LAT), BF),
        V((4, 2, 2, 8, LAT), F32), V((4, 16, LAT), BF), V((4, 16, LAT), BF),
        D((7,)), D((6,)),
        D((2,)), D((1,)), D((6,)), D((6,)), D((8,)), D((8,)), D((8,)), D((8,)),
        D((2,)), D((2,)), D((32,)), D((32,)), D((8,)), D((8,)), D((15,)), D((16,)),
        D((8,)), D((16,)), D((15,)), D((8,)),
        D((20,)), D((20,)), D((20,)), D((20,)),
    ]
    hbm = pl.BlockSpec(memory_space=pl.ANY)
    got = pl.pallas_call(
        kernel,
        out_shape=outs,
        in_specs=[hbm] * 7 + [pl.BlockSpec(memory_space=pltpu.SMEM)],
        out_specs=(hbm,) * 6,
        scratch_shapes=scratch,
        compiler_params=pltpu.CompilerParams(
            collective_id=0, has_side_effects=True, vmem_limit_bytes=62 * 1024 * 1024
        ),
    )(nope, rope, ans.T, *rest)
    res = pl.pallas_call(
        hand_over,
        out_shape=outs,
        in_specs=[hbm] * 6,
        out_specs=(hbm,) * 6,
        scratch_shapes=[V(o.shape, o.dtype) for o in outs] + [D((6,)), D((6,))],
    )(*got)
    return res[0], res[1], res[2].T, res[3], res[4], res[5]


def solution(mesh):
    return jax.shard_map(
        per_device,
        mesh=mesh,
        in_specs=(
            P("ans", "head"),
            P("ans", "head"),
            P("ans", None),
            P("ans", None),
            P("head", None, None),
            P("head", None, None),
            P("ans", "head"),
            P("ans"),
        ),
        out_specs=(
            P("ans", "head"),
            P("ans", "head"),
            P("ans", None),
            P("ans", None),
            P("head", "ans", None),
            P("head", "ans", None),
        ),
        check_vma=False,
    )
```
